32 devices in a mesh: lat: 8 (over y, x, core), dep: 4 (over z).
Axes of the slice: x: 2, y: 2, z: 4, core: 2. Of those that a mesh axis runs over, the one named last changes fastest.
Arguments:
- estimate: float32 [16, 256, 1024], P(None, 'dep', 'lat'), may hold values from -6 to 6
- previous: float32 [16, 256, 1024], P(None, 'dep', 'lat'), may hold values from -6 to 6
- measured: float32 [16, 12, 1024], P('dep', None, 'lat'), may hold values from -21 to 21
- foot_table: bfloat16 [64, 128, 128], replicated, may hold values from -0.01953125 to 0.01953125
- foot_id: int32 [8, 12, 256, 3], P('lat', None, 'dep'), may hold values from 0 to 63
- foot_lo: int32 [8, 12, 256], P('lat', None, 'dep'), may hold values from -1 to 0, as said below
- foot_count: int32 [8, 12, 256], P('lat', None, 'dep'), may hold values from 1 to 3, as said below
- mask_table: float32 [16, 128], replicated, may hold values from 0.2 to 1
- mask_id: int32 [12, 8], P(None, 'lat'), may hold values from 0 to 15
- thresholds: float32 [256], replicated, may hold values from 0.02 to 0.5
Outputs:
- refined: float32 [16, 256, 1024], P(None, 'dep', 'lat')
- extrapolated: float32 [16, 256, 1024], P(None, 'dep', 'lat')
The draws below stay inside these ranges and needn't reach their ends.
Inputs may be any that keep to these rules, and one draw needn't show every extreme that they name: The live offsets foot_lo .. foot_lo + foot_count - 1 of every detector tile, frame and plane lie within -1 .. 1; some entries have foot_lo = -1. `foot_count`: some entries have all three offsets live.
All inputs are finite; a program needn't handle non-finite values.
Results may differ from the reference program's by a relative error of at most 0.00099.
Values may be sent and summed in bfloat16 or wider, within the bound.
No kernel may reach another device: no remote copies, remote signals or barrier semaphores. Data moves between devices by JAX's collectives and lax.ppermute only.
A program may use at most 128 MiB of HBM per device.

```python
import math
import jax
import jax.numpy as jnp
from jax import lax

TILE = 128
PLANES = 256
FRAMES = 12
NROW = 16
FOOTPRINTS = 64
MASKS = 16
ITERS = 2
KSTART = 8
TILES = 8
NCOL = 1024


def footprint_runs(key):
    base = jax.random.fold_in(key, 7)
    shape = (TILES, FRAMES, PLANES)
    first_offset = jax.random.randint(jax.random.fold_in(base, 1), shape, -1, 1)
    run_length = jax.random.randint(jax.random.fold_in(base, 2), shape, 1, 3 - first_offset)
    frame_axis = lax.broadcasted_iota(jnp.int32, shape, 1)
    plane_axis = lax.broadcasted_iota(jnp.int32, shape, 2)
    forced = (frame_axis == 0) & (plane_axis == 0)
    first_offset = jnp.where(forced, -1, first_offset)
    run_length = jnp.where(forced, 3, run_length)
    return (first_offset, run_length)


def draw_foot_lo(key, part):
    return footprint_runs(key)[0]


def draw_foot_count(key, part):
    return footprint_runs(key)[1]


def draw_foot_id(key, part):
    key = jax.random.fold_in(key, 11)
    shape = (TILES, FRAMES, PLANES, 3)
    common_ids = jax.random.randint(jax.random.fold_in(key, 1), (TILES, 1, PLANES, 3), 0, FOOTPRINTS)
    own_ids = jax.random.randint(jax.random.fold_in(key, 2), shape, 0, FOOTPRINTS)
    keep_common = jax.random.randint(jax.random.fold_in(key, 3), shape, 0, 2) == 0
    return jnp.where(keep_common, jnp.broadcast_to(common_ids, shape), own_ids)


def draw_measured(key, part):
    key = jax.random.fold_in(key, 5)
    shape = (NROW, FRAMES, NCOL)
    column = lax.broadcasted_iota(jnp.int32, shape, 2).astype(jnp.float32)
    scale = 1.0 + 2.0 * column / (NCOL - 1)
    shared = jnp.clip(jax.random.normal(jax.random.fold_in(key, 1), (NROW, 1, NCOL), jnp.float32), -5.0, 5.0)
    noise = jnp.clip(jax.random.normal(jax.random.fold_in(key, 2), shape, jnp.float32), -5.0, 5.0)
    return (0.6 * shared + 0.8 * noise) * scale


def plant(values, key, low, top_value):
    longest = values.shape.index(max(values.shape))
    spots = []
    for shift in (0, 1):
        where = [jax.random.randint(jax.random.fold_in(key, axis), (), 0, length) for axis, length in enumerate(values.shape)]
        where[longest] = (where[longest] + shift) % values.shape[longest]
        spots.append(tuple(where))
    return values.at[spots[0]].set(low).at[spots[1]].set(top_value)


def steps_of(own_key, extent, split, low, largest):
    gain, own = 1.0, jax.random.fold_in(own_key, 6)
    for axis_at, parts in split:
        draws = jnp.exp(jax.random.uniform(jax.random.fold_in(own, axis_at), (parts,), jnp.float32, low / len(split), largest / len(split)))
        gain = gain * jnp.repeat(draws, extent[axis_at] // parts).reshape([-1 if axis == axis_at else 1 for axis in range(len(extent))])
    return gain


def normal_values(key, extent, deviation, bound, split=(), held_as=jnp.bfloat16):
    entries = jax.random.normal(key, extent, jnp.float32) * deviation
    if len(split) > 0:
        entries = steps_of(key, extent, split, -0.22, 0.18) * entries
    return jnp.clip(entries, min=-bound, max=bound).astype(held_as)


def setup_inputs(seed: int = 0) -> dict:
    seeds = jax.random.split(jax.random.key(seed), 11)
    return {
        "estimate": normal_values(seeds[0], (NROW, PLANES, NCOL), 1.0, 6.0, ((1, 4), (2, 8)), jnp.float32),
        "previous": normal_values(seeds[1], (NROW, PLANES, NCOL), 1.0, 6.0, ((1, 4), (2, 8)), jnp.float32),
        "measured": draw_measured(jax.random.fold_in(seeds[10], 71), 0),
        "foot_table": normal_values(seeds[3], (FOOTPRINTS, TILE, TILE), (3 * TILE * PLANES) ** -0.5, 0.01953125),
        "foot_id": draw_foot_id(jax.random.fold_in(seeds[10], 71), 0),
        "foot_lo": draw_foot_lo(jax.random.fold_in(seeds[10], 71), 0),
        "foot_count": draw_foot_count(jax.random.fold_in(seeds[10], 71), 0),
        "mask_table": jnp.clip(jnp.exp(jax.random.uniform(seeds[7], (MASKS, TILE), jnp.float32, math.log(0.2), math.log(1.0))), 0.2, 1.0),
        "mask_id": plant(jax.random.randint(seeds[8], (FRAMES, TILES), 0, MASKS), jax.random.fold_in(seeds[8], 1), 0, MASKS - 1).astype(jnp.int32),
        "thresholds": jnp.clip(jnp.exp(jax.random.uniform(seeds[9], (PLANES,), jnp.float32, math.log(0.02), math.log(0.5))), 0.02, 0.5),
    }


root_half = 0.7071067811865476
tiny_eps = 1e-06

def momentum_list():
    ratio_now = 1.0
    ratios = [ratio_now]
    for iteration in range(KSTART + ITERS + 3):
        ratio_now = (1.0 + math.sqrt(1.0 + 4.0 * ratio_now * ratio_now)) / 2.0
        ratios.append(ratio_now)
    return [(ratios[KSTART - 1 + iteration] - 1.0) / ratios[KSTART + iteration] for iteration in range(ITERS + 1)]

def walsh(volume, bit_count):
    row_total, length, tail_size = volume.shape
    for section_bit in range(bit_count):
        stride = 2 ** section_bit
        shaped = volume.reshape(row_total, length // (2 * stride), 2, stride, tail_size)
        lower_half = shaped[:, :, 0]
        higher = shaped[:, :, 1]
        volume = jnp.stack([(lower_half + higher) * root_half, (lower_half - higher) * root_half], axis=2).reshape(row_total, length, tail_size)
    return volume

def footprints(foot_table, foot_id, foot_lo, foot_count, tile_index):
    offsets = jnp.arange(3, dtype=jnp.int32) - 1
    ids = foot_id[tile_index]
    first_offset = foot_lo[tile_index][..., None]
    active = (offsets >= first_offset) & (offsets < first_offset + foot_count[tile_index][..., None])
    chosen = foot_table[ids].astype(jnp.float32)
    return chosen * active[..., None, None].astype(jnp.float32)

def reference(estimate, previous, measured, foot_table, foot_id, foot_lo, foot_count, mask_table, mask_id, thresholds):
    momenta = momentum_list()
    bit_count = PLANES.bit_length() - 1
    mask_rows = mask_table[mask_id].reshape(FRAMES, NCOL)

    def project(lifted):
        padded = jnp.pad(lifted.astype(jnp.float32).reshape(NROW, PLANES, TILES, TILE), ((0, 0), (0, 0), (1, 1), (0, 0)))

        def one_tile(tile_index):
            tile_index = tile_index.astype(jnp.int32)
            neighbours = lax.dynamic_slice_in_dim(padded, tile_index, 3, 2)
            chosen = footprints(foot_table, foot_id, foot_lo, foot_count, tile_index)
            return jnp.einsum('rzoc,fzocd->rfd', neighbours, chosen, precision=lax.Precision.HIGHEST)
        stacked = lax.map(one_tile, jnp.arange(TILES, dtype=jnp.int32))
        return jnp.transpose(stacked, (1, 2, 0, 3)).reshape(NROW, FRAMES, NCOL)

    def back_project(weighted):
        spread = weighted.astype(jnp.float32).reshape(NROW, FRAMES, TILES, TILE)

        def add_tile(tile_index, grad_pad):
            tile_index = tile_index.astype(jnp.int32)
            chosen = footprints(foot_table, foot_id, foot_lo, foot_count, tile_index)
            detector = lax.dynamic_index_in_dim(spread, tile_index, 2, keepdims=False)
            contrib = jnp.einsum('rfd,fzocd->rzoc', detector, chosen, precision=lax.Precision.HIGHEST)
            window = lax.dynamic_slice_in_dim(grad_pad, tile_index, 3, 2)
            return lax.dynamic_update_slice_in_dim(grad_pad, window + contrib, tile_index, 2)
        grad_pad = jnp.zeros((NROW, PLANES, TILES + 2, TILE), jnp.float32)
        grad_pad = lax.fori_loop(0, TILES, add_tile, grad_pad)
        return grad_pad[:, :, 1:-1].reshape(NROW, PLANES, NCOL)
    state = estimate
    current = estimate + momenta[0] * (estimate - previous)
    for iteration in range(ITERS):
        lifted = current.astype(jnp.bfloat16)
        projected = project(lifted)
        residual = mask_rows[None] * projected - measured
        misfit = jnp.sum(residual * residual)
        weighted = (mask_rows[None] * residual).astype(jnp.bfloat16)
        gradient = back_project(weighted)
        grad_sq = jnp.sum(gradient * gradient)
        step_size = 0.5 * misfit / (grad_sq + tiny_eps)
        moved = current - step_size * gradient
        coefficients = walsh(moved, bit_count)
        limit = step_size * thresholds[None, :, None]
        shrunk = coefficients - jnp.clip(coefficients, -limit, limit)
        fresh = walsh(shrunk, bit_count)
        current = fresh + momenta[iteration + 1] * (fresh - state)
        state = fresh
    return (state, current)
```

```python
import functools
import math

import jax
import jax.numpy as jnp
import numpy as np
from jax import lax
from jax.experimental import pallas as pl
from jax.experimental.pallas import tpu as pltpu
from jax.sharding import PartitionSpec as P

ITERS = 2
KSTART = 8

tiny_eps = 1e-06
f32 = jnp.float32
bf16 = jnp.bfloat16

SLOTS = 3


def momentum_list():
    ratio_now = 1.0
    ratios = [ratio_now]
    for iteration in range(KSTART + ITERS + 3):
        ratio_now = (1.0 + math.sqrt(1.0 + 4.0 * ratio_now * ratio_now)) / 2.0
        ratios.append(ratio_now)
    return [
        (ratios[KSTART - 1 + iteration] - 1.0) / ratios[KSTART + iteration]
        for iteration in range(ITERS + 1)
    ]


def signs(length):
    index = np.arange(length)
    both = index[:, None] & index[None]
    parity = np.zeros_like(both)
    while both.any():
        parity ^= both & 1
        both >>= 1
    return np.where(parity == 1, -1.0, 1.0)


def dot(a, b):
    return jnp.dot(a, b, preferred_element_type=f32)


def split_dot(matrix, values):
    upper = values.astype(bf16)
    lower = (values - upper.astype(f32)).astype(bf16)
    return dot(matrix, upper) + dot(matrix, lower)


def call(body, outs, args, prefetch=(), scratch=(), flops=0, limit=28):
    vmem = pl.BlockSpec(memory_space=pltpu.VMEM)
    size = sum(math.prod(a.shape) * a.dtype.itemsize for a in (*args, *outs))
    return pl.pallas_call(
        body,
        out_shape=tuple(outs),
        in_specs=[pl.BlockSpec(memory_space=pltpu.SMEM)] * len(prefetch) + [vmem] * len(args),
        out_specs=tuple([vmem] * len(outs)),
        scratch_shapes=list(scratch),
        compiler_params=pltpu.CompilerParams(vmem_limit_bytes=limit * 2**20),
        cost_estimate=pl.CostEstimate(flops=flops, bytes_accessed=size, transcendentals=0),
    )(*prefetch, *args)


def shape(dims, dtype):
    return jax.ShapeDtypeStruct(tuple(dims), dtype)


def prepare_kernel(count, rows, momentum, me_ref, est_ref, prev_ref, *outs):
    heads, rests = outs[:count], outs[count:]
    for slot in range(count):
        group = pl.ds((me_ref[0] ^ slot) * rows, rows)
        est = est_ref[group]
        current = est + momentum * (est - prev_ref[group])
        head = current.astype(bf16)
        heads[slot][...] = head
        rests[slot][0] = (current - head.astype(f32)).astype(bf16)
        upper = est.astype(bf16)
        rests[slot][1] = upper
        rests[slot][2] = (est - upper.astype(f32)).astype(bf16)


def choose_kernel(count, block, prints, *refs):
    ids, choose_ref = refs[:count], refs[count]
    wide = jnp.concatenate([r[...] for r in ids], axis=1)
    for pair in range(prints // 2):
        both = jnp.concatenate(
            [jnp.where(wide == 2 * pair + k, 1.0, 0.0).astype(f32) for k in (0, 1)], axis=0
        )
        choose_ref[pl.ds(pair * 2 * block, 2 * block)] = both.astype(bf16)


def choose_t_kernel(count, block, prints, spread_ref, number_ref, *refs):
    ids, choose_ref = refs[:count], refs[count]
    wide = jnp.concatenate([r[...] for r in ids], axis=1).astype(f32)
    tall = wide.T.astype(bf16)
    step = 5 * 128
    width = prints * block
    for start in range(0, width, step):
        stop = min(start + step, width)
        lanes = dot(tall, spread_ref[:, start:stop])
        choose_ref[:, start:stop] = jnp.where(lanes == number_ref[0:1, start:stop], 1.0, 0.0).astype(bf16)


def project(rows, block, frames, prints, lifted, choose_ref, table_ref, acc_ref, outs):
    per = 8 if prints % 8 == 0 else 2
    tile = table_ref.shape[1]
    total = jnp.zeros((rows * block, tile), f32)
    for start in range(0, prints, per):
        summed = dot(choose_ref[pl.ds(start * block, per * block)], lifted)
        for pair in range(per // 2):
            base = 2 * pair * block
            left = jnp.concatenate(
                [
                    jnp.concatenate(
                        [
                            summed[base + k * block : base + (k + 1) * block, r * tile : (r + 1) * tile]
                            for k in (0, 1)
                        ],
                        axis=1,
                    )
                    for r in range(rows)
                ],
                axis=0,
            )
            upper = left.astype(bf16)
            lower = (left - upper.astype(f32)).astype(bf16)
            weights = table_ref[pl.ds(start + 2 * pair, 2)].reshape(2 * tile, tile)
            total = total + dot(upper, weights) + dot(lower, weights)
    acc_ref[...] = total
    for slot in range(SLOTS):
        for r in range(rows):
            outs[slot][r] = acc_ref[pl.ds(r * block + slot * frames, frames)]


def project_kernel(count, rows, block, frames, prints, *refs):
    heads = refs[:count]
    choose_ref, table_ref = refs[count : count + 2]
    outs = refs[count + 2 : count + 2 + SLOTS]
    acc_ref = refs[count + 2 + SLOTS]
    lifted = jnp.concatenate(
        [jnp.concatenate([h[r] for r in range(rows)], axis=1) for h in heads], axis=0
    )
    project(rows, block, frames, prints, lifted, choose_ref, table_ref, acc_ref, outs)


def residual_kernel(frames, id_ref, own_ref, a_ref, b_ref, measured_ref, masks_ref, w_ref, misfit_ref, mask_ref):
    for f in range(frames):
        mask_ref[pl.ds(f, 1)] = masks_ref[pl.ds(id_ref[f], 1)]
    mask = mask_ref[...]
    total = jnp.zeros((1, mask.shape[1]), f32)
    for r in range(own_ref.shape[0]):
        projected = own_ref[r] + (a_ref[r] + b_ref[r])
        residual = mask * projected - measured_ref[r]
        total = total + jnp.sum(residual * residual, axis=0, keepdims=True)
        w_ref[r] = (mask * residual).astype(bf16)
    misfit_ref[...] = total


def back_kernel(
    rows, block, frames, prints, own_ref, a_ref, b_ref, choose_ref, table_ref, misfit_ref,
    grad_ref, sums_ref, left_ref, upper_ref, lower_ref,
):
    tile = table_ref.shape[1]
    left_ref[...] = jnp.zeros_like(left_ref)
    for slot, ref in enumerate((own_ref, a_ref, b_ref)):
        for r in range(rows):
            left_ref[pl.ds(r * block + slot * frames, frames)] = ref[r].astype(f32)
    left = left_ref[...].astype(bf16)
    per = 8 if prints % 8 == 0 else 2
    for start in range(0, prints, per):
        weights = table_ref[pl.ds(start, per)].reshape(per * tile, tile)
        spread = lax.dot_general(left, weights, (((1,), (1,)), ((), ())), preferred_element_type=f32)
        for pair in range(per // 2):
            both = jnp.concatenate(
                [
                    jnp.concatenate(
                        [
                            spread[r * block : (r + 1) * block, k * tile : (k + 1) * tile]
                            for r in range(rows)
                        ],
                        axis=1,
                    )
                    for k in (2 * pair, 2 * pair + 1)
                ],
                axis=0,
            )
            upper = both.astype(bf16)
            where = pl.ds((start + 2 * pair) * block, 2 * block)
            upper_ref[where] = upper
            lower_ref[where] = (both - upper.astype(f32)).astype(bf16)
    choose = choose_ref[...]
    gradient = dot(choose, upper_ref[...]) + dot(choose, lower_ref[...])
    grad_ref[...] = gradient
    grad_sum = jnp.sum(jnp.sum(gradient * gradient, axis=0, keepdims=True), axis=1, keepdims=True)
    misfit_sum = jnp.sum(misfit_ref[...], axis=1, keepdims=True)
    lane = lax.broadcasted_iota(jnp.int32, sums_ref.shape, 1)
    sums_ref[...] = jnp.where(lane < sums_ref.shape[1] // 2, misfit_sum, grad_sum)


def shrink(scale, sums_ref, current, grad, had_ref, limits_ref):
    total = jnp.sum(sums_ref[...], axis=0, keepdims=True)
    half = total.shape[1] // 2
    step = 0.5 * total[:, 0:1] / (total[:, half : half + 1] + tiny_eps)
    moved = current - step * grad
    coefficients = split_dot(had_ref[...], moved) * scale
    limit = step * limits_ref[...]
    limit = jnp.concatenate([limit] * (moved.shape[1] // limit.shape[1]), axis=1)
    clipped = jnp.clip(coefficients, -limit, limit)
    return moved - split_dot(had_ref[...], clipped) * scale


def first_kernel(count, rows, block, frames, prints, scale, momentum, *refs):
    heads, refs = refs[:count], refs[count:]
    rests, refs = refs[:count], refs[count:]
    sums_ref, grad_ref, had_ref, limits_ref, choose_ref, table_ref = refs[:6]
    outs, refs = refs[6 : 6 + SLOTS], refs[6 + SLOTS :]
    current_ref, refs = refs[0], refs[1:]
    fresh_refs, acc_ref = refs[:count], refs[count]

    def whole(piece):
        return jnp.concatenate(
            [jnp.concatenate([piece(s, r) for r in range(rows)], axis=1) for s in range(count)], axis=0
        )

    current = whole(lambda s, r: heads[s][r].astype(f32) + rests[s][0, r].astype(f32))
    state = whole(lambda s, r: rests[s][1, r].astype(f32) + rests[s][2, r].astype(f32))
    fresh = shrink(scale, sums_ref, current, grad_ref[...], had_ref, limits_ref)
    put_slots(fresh, fresh_refs, rows)
    current = fresh + momentum * (fresh - state)
    current_ref[...] = current
    project(rows, block, frames, prints, current.astype(bf16), choose_ref, table_ref, acc_ref, outs)


def put_slots(fresh, refs, rows):
    depth, tile = refs[0].shape[1:]
    for slot, ref in enumerate(refs):
        for r in range(rows):
            ref[r] = fresh[slot * depth : (slot + 1) * depth, r * tile : (r + 1) * tile]


def last_kernel(count, rows, scale, sums_ref, current_ref, grad_ref, had_ref, limits_ref, *fresh_refs):
    fresh = shrink(scale, sums_ref, current_ref[...], grad_ref[...], had_ref, limits_ref)
    put_slots(fresh, fresh_refs, rows)


def finish_kernel(count, rows, momentum, me_ref, *refs):
    states, fresh, (refined_ref, ahead_ref) = refs[:count], refs[count : 2 * count], refs[2 * count :]
    for slot in range(count):
        group = pl.ds((me_ref[0] ^ slot) * rows, rows)
        now = fresh[slot][...]
        refined_ref[group] = now
        ahead_ref[group] = now + momentum * (now - states[slot][...])


def depth_exchange(parts):
    count = len(parts)
    return [parts[0]] + [
        lax.ppermute(parts[s], "dep", [(i, i ^ s) for i in range(count)]) for s in range(1, count)
    ]


def partner_exchange(to_a, to_b):
    count = lax.axis_size("lat")
    pairs_a = [(i, i ^ 1) for i in range(count)]
    pairs_b = [(i, (i + 1 if i % 2 else i - 1) % count) for i in range(count)]
    return lax.ppermute(to_a, "lat", pairs_a), lax.ppermute(to_b, "lat", pairs_b)


def local(
    estimate,
    previous,
    measured,
    foot_table,
    foot_id,
    foot_lo,
    foot_count,
    mask_table,
    mask_id,
    thresholds,
):
    row_total, depth_local, tile = estimate.shape
    count = lax.axis_size("dep")
    lat_count = lax.axis_size("lat")
    rows = row_total // count
    depth = depth_local * count
    frames = measured.shape[1]
    prints = foot_table.shape[0]
    block = -(-SLOTS * frames // 8) * 8
    width = rows * tile
    momenta = momentum_list()
    scale = float(0.7071067811865476 ** (depth.bit_length() - 1))
    had = jnp.asarray(signs(depth), bf16)
    limits = jnp.broadcast_to(thresholds[:, None], (depth, tile))
    place = lax.axis_index("lat")
    me = lax.axis_index("dep").astype(jnp.int32).reshape(1)
    volume = shape((rows, depth_local, tile), f32)

    offsets = (jnp.arange(3, dtype=jnp.int32) - 1)[None, :, None]
    first = foot_lo[0][:, None]
    live = (offsets >= first) & (offsets < first + foot_count[0][:, None])
    ids = jnp.where(live, jnp.transpose(foot_id[0], (0, 2, 1)), -1)
    odd = place % 2 == 1
    lower, upper = ids[:, 0], ids[:, 2]
    ids_a, ids_b = partner_exchange(jnp.where(odd, lower, upper), jnp.where(odd, upper, lower))
    ids_b = jnp.where((place == 0) | (place == lat_count - 1), -1, ids_b)
    pad = jnp.full((block - SLOTS * frames, depth_local), -1, jnp.int32)
    ids = depth_exchange([jnp.concatenate([ids[:, 1], ids_a, ids_b, pad], axis=0)] * count)

    prepared = call(
        functools.partial(prepare_kernel, count, rows, momenta[0]),
        [shape((rows, depth_local, tile), bf16)] * count + [shape((3, rows, depth_local, tile), bf16)] * count,
        [estimate, previous],
        prefetch=[me],
    )
    heads = depth_exchange(prepared[:count])
    rests = depth_exchange(prepared[count:])

    (choose,) = call(
        functools.partial(choose_kernel, count, block, prints), [shape((prints * block, depth), bf16)], ids
    )
    lanes = np.arange(prints * block)
    spread = jnp.asarray(lanes[None] % block == np.arange(block)[:, None], bf16)
    number = jnp.asarray(np.broadcast_to(lanes // block, (8, prints * block)), f32)
    (choose_t,) = call(
        functools.partial(choose_t_kernel, count, block, prints),
        [shape((depth, prints * block), bf16)],
        [spread, number, *ids],
    )
    sizes = (count, rows, block, frames, prints)
    acc = pltpu.VMEM((rows * block, tile), f32)
    part = shape((rows, frames, tile), f32)
    work = 2 * prints * block * width * (depth + tile)
    parts = call(
        functools.partial(project_kernel, *sizes),
        [part] * SLOTS,
        [*heads, choose, foot_table],
        scratch=[acc],
        flops=work,
    )

    def step_sums(parts):
        part_a, part_b = partner_exchange(parts[1], parts[2])
        weighted, misfit = call(
            functools.partial(residual_kernel, frames),
            [shape((rows, frames, tile), bf16), shape((1, tile), f32)],
            [parts[0], part_a, part_b, measured, mask_table],
            prefetch=[mask_id[:, 0]],
            scratch=[pltpu.VMEM((frames, tile), f32)],
        )
        weighted_a, weighted_b = partner_exchange(weighted, weighted)
        gradient, sums = call(
            functools.partial(back_kernel, *sizes[1:]),
            [shape((depth, width), f32), shape((count * lat_count, tile), f32)],
            [weighted, weighted_a, weighted_b, choose_t, foot_table, misfit],
            scratch=[
                pltpu.VMEM((rows * block, tile), f32),
                pltpu.VMEM((prints * block, width), bf16),
                pltpu.VMEM((prints * block, width), bf16),
            ],
            flops=2 * work,
        )
        return gradient, lax.all_to_all(sums, ("lat", "dep"), split_axis=0, concat_axis=0, tiled=True)

    gradient, sums = step_sums(parts)
    done = call(
        functools.partial(first_kernel, *sizes, scale, momenta[1]),
        [part] * SLOTS + [shape((depth, width), f32)] + [volume] * count,
        [*heads, *rests, sums, gradient, had, limits, choose, foot_table],
        scratch=[acc],
        flops=work,
    )
    parts, current, states = done[:SLOTS], done[SLOTS], depth_exchange(done[SLOTS + 1 :])
    gradient, sums = step_sums(parts)
    fresh = depth_exchange(
        call(
            functools.partial(last_kernel, count, rows, scale),
            [volume] * count,
            [sums, current, gradient, had, limits],
        )
    )
    return call(
        functools.partial(finish_kernel, count, rows, momenta[2]),
        [shape(estimate.shape, f32)] * 2,
        [*states, *fresh],
        prefetch=[me],
    )


def solution(mesh):
    in_specs = (
        P(None, "dep", "lat"),
        P(None, "dep", "lat"),
        P("dep", None, "lat"),
        P(),
        P("lat", None, "dep", None),
        P("lat", None, "dep"),
        P("lat", None, "dep"),
        P(),
        P(None, "lat"),
        P(),
    )
    out_specs = (P(None, "dep", "lat"), P(None, "dep", "lat"))
    return jax.shard_map(local, mesh=mesh, in_specs=in_specs, out_specs=out_specs, check_vma=False)
```

```python
import functools
import math

import jax
import jax.numpy as jnp
import numpy as np
from jax import lax
from jax.experimental import pallas as pl
from jax.experimental.pallas import tpu as pltpu
from jax.sharding import PartitionSpec as P

ITERS = 2
KSTART = 8

tiny_eps = 1e-06
f32 = jnp.float32
bf16 = jnp.bfloat16

SLOTS = 3
LEVELS = 32700.0


def momentum_list():
    ratio_now = 1.0
    ratios = [ratio_now]
    for iteration in range(KSTART + ITERS + 3):
        ratio_now = (1.0 + math.sqrt(1.0 + 4.0 * ratio_now * ratio_now)) / 2.0
        ratios.append(ratio_now)
    return [
        (ratios[KSTART - 1 + iteration] - 1.0) / ratios[KSTART + iteration]
        for iteration in range(ITERS + 1)
    ]


def signs(length):
    index = np.arange(length)
    both = index[:, None] & index[None]
    parity = np.zeros_like(both)
    while both.any():
        parity ^= both & 1
        both >>= 1
    return np.where(parity == 1, -1.0, 1.0)


def dot(a, b):
    return jnp.dot(a, b, preferred_element_type=f32)


def split_dot(matrix, values):
    upper = values.astype(bf16)
    lower = (values - upper.astype(f32)).astype(bf16)
    return dot(matrix, upper) + dot(matrix, lower)


def call(body, outs, args, prefetch=(), scratch=(), flops=0, limit=28, far=(), far_outs=False, anchors=()):
    vmem = pl.BlockSpec(memory_space=pltpu.VMEM)
    hbm = pl.BlockSpec(memory_space=pltpu.HBM)
    ahead = [pl.BlockSpec(memory_space=pl.ANY)] * len(anchors)
    size = sum(math.prod(a.shape) * a.dtype.itemsize for a in (*args, *outs, *far))
    return pl.pallas_call(
        body,
        out_shape=tuple(outs),
        in_specs=[pl.BlockSpec(memory_space=pltpu.SMEM)] * len(prefetch) + ahead + [vmem] * len(args) + [hbm] * len(far),
        out_specs=tuple([hbm if far_outs else vmem] * len(outs)),
        scratch_shapes=list(scratch),
        compiler_params=pltpu.CompilerParams(vmem_limit_bytes=limit * 2**20),
        cost_estimate=pl.CostEstimate(flops=flops, bytes_accessed=size, transcendentals=0),
    )(*prefetch, *anchors, *args, *far)


def shape(dims, dtype):
    return jax.ShapeDtypeStruct(tuple(dims), dtype)


def encode(ref, values):
    rows, depth, tile = values.shape
    flat = jnp.concatenate([values[r] for r in range(rows)], axis=0)
    bound = jnp.max(jnp.max(jnp.abs(flat), axis=0, keepdims=True), axis=1, keepdims=True)
    exponent = jnp.floor(jnp.log2(jnp.maximum(bound, 1e-30))) + 1.0
    coded = jnp.clip(jnp.round(flat * (LEVELS * jnp.exp2(-exponent))), -32767.0, 32767.0)
    ref[pl.ds(0, rows * depth)] = coded.astype(jnp.int32).astype(jnp.int16)
    ref[pl.ds(rows * depth, 16)] = jnp.broadcast_to(exponent, (16, tile)).astype(jnp.int32).astype(jnp.int16)


def decode(ref, size):
    coded = ref[pl.ds(0, size + 16)].astype(jnp.int32).astype(f32)
    return coded[:size] * (jnp.exp2(coded[size : size + 1, 0:1]) * (1.0 / LEVELS))


def decode_wide(refs, rows, depth):
    pieces = [decode(ref, rows * depth) for ref in refs]
    return jnp.concatenate(
        [jnp.concatenate([p[r * depth : (r + 1) * depth] for r in range(rows)], axis=1) for p in pieces],
        axis=0,
    )


def lateral_kernel(rows, frames, mask_ref, *refs):
    outs, held, sems = refs[5:8], refs[8:13], refs[13]
    copies = [pltpu.make_async_copy(a, b, sems.at[i]) for i, (a, b) in enumerate(zip(refs[:5], held))]
    for copy in copies:
        copy.start()
    id_ref, lo_ref, live_ref, measured_ref, masks_ref = held
    odd = lax.axis_index("lat") % 2 == 1
    own_ref = outs[0]
    depth = id_ref.shape[3]
    for ref in outs:
        ref[rows + 1] = jnp.full(ref.shape[1:], -1.0, f32)
    for copy in copies:
        copy.wait()
    for f in range(frames):
        first = lo_ref[f]
        end = first + live_ref[f]
        ids = [jnp.where((o - 1 >= first) & (o - 1 < end), id_ref[f, o], -1).astype(f32) for o in range(3)]
        for ref, row in zip(outs, (ids[1], jnp.where(odd, ids[0], ids[2]), jnp.where(odd, ids[2], ids[0]))):
            ref[rows + 1, pl.ds(f, 1), pl.ds(0, depth)] = row
        own_ref[rows, pl.ds(f, 1)] = masks_ref[pl.ds(mask_ref[f], 1)]
        for r in range(rows):
            own_ref[r, pl.ds(f, 1)] = measured_ref[f, pl.ds(r, 1)]
    for ref in outs[1:]:
        ref[pl.ds(0, rows + 1)] = own_ref[pl.ds(0, rows + 1)]


def prepare_kernel(count, rows, momentum, est_ref, prev_ref, *refs):
    me = lax.axis_index("dep")
    for slot in range(count):
        group = pl.ds((me ^ slot) * rows, rows)
        est = est_ref[group]
        encode(refs[slot], est + momentum * (est - prev_ref[group]))
        encode(refs[count + slot], est)


def fill_kernel(count, rows, frames, own_ref, a_ref, b_ref, *refs):
    ids_ref = refs[2 * count]
    place, last = lax.axis_index("lat"), lax.axis_size("lat") - 1
    ids_ref[...] = jnp.full(ids_ref.shape, -1.0, f32)
    ids_ref[pl.ds(0, frames)] = own_ref[rows + 1]
    ids_ref[pl.ds(frames, frames)] = a_ref[rows + 1]
    ids_ref[pl.ds(2 * frames, frames)] = jnp.where((place == 0) | (place == last), -1.0, b_ref[rows + 1])
    ids = ids_ref[...].astype(jnp.int32).astype(jnp.int16)
    for coded, out in zip(refs[:count], refs[count : 2 * count]):
        size = coded.shape[0]
        out[pl.ds(0, size)] = coded[...]
        out[pl.ds(size, ids.shape[0])] = ids


def table_kernel(anchor_ref, table_ref, out_ref):
    out_ref[...] = table_ref[...]


def state_kernel(rows, tile, fresh_ref, *refs):
    put_slots(fresh_ref[...], refs, rows, tile)


def choose_t_kernel(block, prints, spread_ref, number_ref, ids_ref, choose_ref):
    tall = ids_ref[...].T.astype(bf16)
    step = 5 * 128
    width = prints * block
    for start in range(0, width, step):
        stop = min(start + step, width)
        lanes = dot(tall, spread_ref[:, start:stop])
        choose_ref[:, start:stop] = jnp.where(lanes == number_ref[0:1, start:stop], 1.0, 0.0).astype(bf16)


def project(rows, block, frames, prints, lifted, choose_ref, table_ref, acc_ref, outs):
    per = 8 if prints % 8 == 0 else 2
    tile = table_ref.shape[1]
    total = jnp.zeros((rows * block, tile), f32)
    for start in range(0, prints, per):
        summed = dot(choose_ref[pl.ds(start * block, per * block)], lifted)
        for pair in range(per // 2):
            base = 2 * pair * block
            left = jnp.concatenate(
                [
                    jnp.concatenate(
                        [
                            summed[base + k * block : base + (k + 1) * block, r * tile : (r + 1) * tile]
                            for k in (0, 1)
                        ],
                        axis=1,
                    )
                    for r in range(rows)
                ],
                axis=0,
            )
            upper = left.astype(bf16)
            lower = (left - upper.astype(f32)).astype(bf16)
            weights = table_ref[pl.ds(start + 2 * pair, 2)].reshape(2 * tile, tile)
            total = total + dot(upper, weights) + dot(lower, weights)
    acc_ref[...] = total
    to_a_ref, to_b_ref, part_a_ref, part_b_ref = outs
    for r in range(rows):
        own, part_a, part_b = (acc_ref[pl.ds(r * block + slot * frames, frames)] for slot in range(SLOTS))
        to_a_ref[r] = own
        to_a_ref[rows + r] = part_a
        part_a_ref[r] = part_a
        to_b_ref[r] = own
        to_b_ref[rows + r] = part_b
        part_b_ref[r] = part_b


def project_kernel(count, rows, block, frames, prints, depth, *refs):
    currents, table_ref, outs = refs[:count], refs[count], refs[count + 1 : count + 5]
    choose_ref, ids_ref, acc_ref = refs[count + 5 :]
    top = rows * depth + 16
    rest = currents[0].shape[0] - top
    wide = jnp.concatenate(
        [c[pl.ds(top, rest)].astype(jnp.int32).astype(f32)[:block, :depth] for c in currents], axis=1
    )
    ids_ref[...] = wide
    for pair in range(prints // 2):
        both = jnp.concatenate(
            [jnp.where(wide == float(2 * pair + k), 1.0, 0.0).astype(f32) for k in (0, 1)], axis=0
        )
        choose_ref[pl.ds(pair * 2 * block, 2 * block)] = both.astype(bf16)
    lifted = decode_wide(currents, rows, depth).astype(bf16)
    project(rows, block, frames, prints, lifted, choose_ref, table_ref, acc_ref, outs)


def back_kernel(
    skip, rows, block, frames, prints, *refs
):
    own_ref, a_ref, b_ref, to_a_ref, part_b_ref, from_a_ref, from_b_ref, past_a_ref, past_b_ref = refs[skip : skip + 9]
    choose_ref, table_ref, grad_ref, sums_ref, left_ref, upper_ref, lower_ref = refs[skip + 9 :]
    tile = table_ref.shape[1]
    left_ref[...] = jnp.zeros_like(left_ref)
    misfit = jnp.zeros((1, tile), f32)
    for r in range(rows):
        projected = (
            to_a_ref[r] + (from_a_ref[rows + r] + from_b_ref[rows + r]),
            from_a_ref[r] + (to_a_ref[rows + r] + past_a_ref[r]),
            from_b_ref[r] + (part_b_ref[r] + past_b_ref[r]),
        )
        for slot, ref in enumerate((own_ref, a_ref, b_ref)):
            mask = ref[rows]
            residual = mask * projected[slot] - ref[r]
            if slot == 0:
                misfit = misfit + jnp.sum(residual * residual, axis=0, keepdims=True)
            weighted = (mask * residual).astype(bf16).astype(f32)
            left_ref[pl.ds(r * block + slot * frames, frames)] = weighted
    left = left_ref[...].astype(bf16)
    per = 8 if prints % 8 == 0 else 2
    for start in range(0, prints, per):
        weights = table_ref[pl.ds(start, per)].reshape(per * tile, tile)
        spread = lax.dot_general(left, weights, (((1,), (1,)), ((), ())), preferred_element_type=f32)
        for pair in range(per // 2):
            both = jnp.concatenate(
                [
                    jnp.concatenate(
                        [
                            spread[r * block : (r + 1) * block, k * tile : (k + 1) * tile]
                            for r in range(rows)
                        ],
                        axis=1,
                    )
                    for k in (2 * pair, 2 * pair + 1)
                ],
                axis=0,
            )
            upper = both.astype(bf16)
            where = pl.ds((start + 2 * pair) * block, 2 * block)
            upper_ref[where] = upper
            lower_ref[where] = (both - upper.astype(f32)).astype(bf16)
    choose = choose_ref[...]
    gradient = dot(choose, upper_ref[...]) + dot(choose, lower_ref[...])
    grad_ref[...] = gradient
    grad_sum = jnp.sum(jnp.sum(gradient * gradient, axis=0, keepdims=True), axis=1, keepdims=True)
    misfit_sum = jnp.sum(misfit, axis=1, keepdims=True)
    lane = lax.broadcasted_iota(jnp.int32, sums_ref.shape, 1)
    sums_ref[...] = jnp.where(lane < sums_ref.shape[1] // 2, misfit_sum, grad_sum)


def shrink(scale, sums_ref, current, grad, had_ref, limits_ref):
    total = jnp.sum(sums_ref[...], axis=0, keepdims=True)
    half = total.shape[1] // 2
    step = 0.5 * total[:, 0:1] / (total[:, half : half + 1] + tiny_eps)
    moved = current - step * grad
    coefficients = split_dot(had_ref[...], moved) * scale
    limit = step * limits_ref[...]
    limit = jnp.concatenate([limit] * (moved.shape[1] // limit.shape[1]), axis=1)
    clipped = jnp.clip(coefficients, -limit, limit)
    return moved - split_dot(had_ref[...], clipped) * scale


def first_kernel(count, rows, block, frames, prints, depth, scale, momentum, *refs):
    currents, refs = refs[:count], refs[count:]
    states, refs = refs[:count], refs[count:]
    sums_ref, grad_ref, had_ref, limits_ref, choose_ref, table_ref = refs[:6]
    outs, refs = refs[6:10], refs[10:]
    current_ref, fresh_ref, acc_ref = refs

    current, state = decode_wide(currents, rows, depth), decode_wide(states, rows, depth)
    fresh = shrink(scale, sums_ref, current, grad_ref[...], had_ref, limits_ref)
    fresh_ref[...] = fresh
    current = fresh + momentum * (fresh - state)
    current_ref[...] = current
    project(rows, block, frames, prints, current.astype(bf16), choose_ref, table_ref, acc_ref, outs)


def put_slots(fresh, refs, rows, tile):
    depth = fresh.shape[0] // len(refs)
    for slot in [*range(1, len(refs)), 0]:
        piece = fresh[slot * depth : (slot + 1) * depth]
        encode(refs[slot], jnp.stack([piece[:, r * tile : (r + 1) * tile] for r in range(rows)]))


def last_kernel(count, rows, scale, sums_ref, current_ref, grad_ref, had_ref, limits_ref, *fresh_refs):
    tile = limits_ref.shape[1]
    fresh = shrink(scale, sums_ref, current_ref[...], grad_ref[...], had_ref, limits_ref)
    put_slots(fresh, fresh_refs, rows, tile)


def finish_kernel(count, rows, momentum, *refs):
    states, fresh = refs[:count], refs[count : 2 * count]
    refined_hbm, ahead_hbm, refined_ref, ahead_ref, sems = refs[2 * count :]
    me = lax.axis_index("dep")
    copies = []
    for slot in range(count):
        group = pl.ds((me ^ slot) * rows, rows)
        size = math.prod(refined_ref.shape[1:3])
        now, before = decode(fresh[slot], size), decode(states[slot], size)
        refined_ref[slot] = now.reshape(refined_ref.shape[1:])
        ahead_ref[slot] = (now + momentum * (now - before)).reshape(ahead_ref.shape[1:])
        copies.append(pltpu.make_async_copy(refined_ref.at[slot], refined_hbm.at[group], sems.at[0, slot]))
        copies.append(pltpu.make_async_copy(ahead_ref.at[slot], ahead_hbm.at[group], sems.at[1, slot]))
        copies[-2].start()
        copies[-1].start()
    for copy in copies:
        copy.wait()


def depth_exchange(parts):
    count = len(parts)
    return [parts[0]] + [
        lax.ppermute(parts[s], "dep", [(i, i ^ s) for i in range(count)]) for s in range(1, count)
    ]


def partner_exchange(to_a, to_b):
    count = lax.axis_size("lat")
    pairs_a = [(i, i ^ 1) for i in range(count)]
    pairs_b = [(i, (i + 1 if i % 2 else i - 1) % count) for i in range(count)]
    return lax.ppermute(to_a, "lat", pairs_a), lax.ppermute(to_b, "lat", pairs_b)


def past_exchange(part_a, part_b):
    count = lax.axis_size("lat")
    past_a = [(i, (i + 2 if i % 2 else i - 2) % count) for i in range(count)]
    past_b = [(i, (i - 2 if i % 2 else i + 2) % count) for i in range(count)]
    return lax.ppermute(part_b, "lat", past_a), lax.ppermute(part_a, "lat", past_b)


def local(
    estimate,
    previous,
    measured,
    foot_table,
    foot_id,
    foot_lo,
    foot_count,
    mask_table,
    mask_id,
    thresholds,
):
    row_total, depth_local, tile = estimate.shape
    count = lax.axis_size("dep")
    lat_count = lax.axis_size("lat")
    rows = row_total // count
    depth = depth_local * count
    frames = measured.shape[1]
    prints = foot_table.shape[0]
    block = -(-SLOTS * frames // 8) * 8
    width = rows * tile
    momenta = momentum_list()
    scale = float(0.7071067811865476 ** (depth.bit_length() - 1))
    had = jnp.asarray(signs(depth), bf16)
    limits = jnp.broadcast_to(thresholds[:, None], (depth, tile))
    volume = (rows, depth_local, tile)
    coded = shape((rows * depth_local + 16, tile), jnp.int16)

    small = [
        jnp.transpose(foot_id, (1, 3, 0, 2)),
        jnp.transpose(foot_lo, (1, 0, 2)),
        jnp.transpose(foot_count, (1, 0, 2)),
        jnp.transpose(measured, (1, 0, 2)),
        mask_table,
    ]
    pack = shape((rows + 2, frames, tile), f32)
    own, to_a, to_b = call(
        functools.partial(lateral_kernel, rows, frames),
        [pack] * 3,
        [],
        far=small,
        scratch=[*(pltpu.VMEM(a.shape, a.dtype) for a in small), pltpu.SemaphoreType.DMA((len(small),))],
        prefetch=[mask_id[:, 0]],
        limit=56,
    )
    packs = [own, *partner_exchange(to_a, to_b)]

    more = -(-block // 16) * 16
    prepared = call(
        functools.partial(prepare_kernel, count, rows, momenta[0]), [coded] * (2 * count), [estimate, previous]
    )
    currents = call(
        functools.partial(fill_kernel, count, rows, frames),
        [shape((rows * depth_local + 16 + more, tile), jnp.int16)] * count,
        [*packs, *prepared[:count]],
        scratch=[pltpu.VMEM((more, tile), f32)],
    )
    (table,) = call(
        table_kernel,
        [shape(foot_table.shape, foot_table.dtype)],
        [foot_table],
        anchors=currents[:1],
    )
    currents = depth_exchange(currents)
    states = depth_exchange(prepared[count:])
    lanes = np.arange(prints * block)
    spread = jnp.asarray(lanes[None] % block == np.arange(block)[:, None], bf16)
    number = jnp.asarray(np.broadcast_to(lanes // block, (8, prints * block)), f32)
    sizes = (rows, block, frames, prints)
    acc = pltpu.VMEM((rows * block, tile), f32)
    part, double = shape((rows, frames, tile), f32), shape((2 * rows, frames, tile), f32)
    work = 2 * prints * block * width * (depth + tile)
    *parts, choose, ids = call(
        functools.partial(project_kernel, count, *sizes, depth_local),
        [double, double, part, part, shape((prints * block, depth), bf16), shape((block, depth), f32)],
        [*currents, table],
        scratch=[acc],
        flops=work,
    )
    (choose_t,) = call(
        functools.partial(choose_t_kernel, block, prints),
        [shape((depth, prints * block), bf16)],
        [spread, number, ids],
    )

    def step_sums(parts, hidden):
        to_a, to_b, part_a, part_b = parts
        gradient, sums = call(
            functools.partial(back_kernel, len(hidden), *sizes),
            [shape((depth, width), f32), shape((count * lat_count, tile), f32)],
            [
                *packs,
                to_a,
                part_b,
                *partner_exchange(to_a, to_b),
                *past_exchange(part_a, part_b),
                choose_t,
                table,
            ],
            scratch=[
                pltpu.VMEM((rows * block, tile), f32),
                pltpu.VMEM((prints * block, width), bf16),
                pltpu.VMEM((prints * block, width), bf16),
            ],
            flops=2 * work,
            anchors=hidden,
        )
        return gradient, lax.all_to_all(sums, ("lat", "dep"), split_axis=0, concat_axis=0, tiled=True)

    gradient, sums = step_sums(parts, states[1:])
    done = call(
        functools.partial(first_kernel, count, *sizes, depth_local, scale, momenta[1]),
        [double, double, part, part] + [shape((depth, width), f32)] * 2,
        [*currents, *states, sums, gradient, had, limits, choose, table],
        scratch=[acc],
        flops=work,
    )
    parts, current = done[:4], done[4]
    states = depth_exchange(
        call(functools.partial(state_kernel, rows, tile), [coded] * count, [done[5]])
    )
    gradient, sums = step_sums(parts, [])
    fresh = depth_exchange(
        call(
            functools.partial(last_kernel, count, rows, scale),
            [coded] * count,
            [sums, current, gradient, had, limits],
        )
    )
    return call(
        functools.partial(finish_kernel, count, rows, momenta[2]),
        [shape(estimate.shape, f32)] * 2,
        [*states, *fresh],
        far_outs=True,
        scratch=[
            pltpu.VMEM((count, *volume), f32),
            pltpu.VMEM((count, *volume), f32),
            pltpu.SemaphoreType.DMA((2, count)),
        ],
    )


def solution(mesh):
    in_specs = (
        P(None, "dep", "lat"),
        P(None, "dep", "lat"),
        P("dep", None, "lat"),
        P(),
        P("lat", None, "dep", None),
        P("lat", None, "dep"),
        P("lat", None, "dep"),
        P(),
        P(None, "lat"),
        P(),
    )
    out_specs = (P(None, "dep", "lat"), P(None, "dep", "lat"))
    return jax.shard_map(local, mesh=mesh, in_specs=in_specs, out_specs=out_specs, check_vma=False)
```

```python
import functools
import math

import jax
import jax.numpy as jnp
import numpy as np
from jax import lax
from jax.experimental import pallas as pl
from jax.experimental.pallas import tpu as pltpu
from jax.sharding import PartitionSpec as P

ITERS = 2
KSTART = 8

tiny_eps = 1e-06
f32 = jnp.float32
bf16 = jnp.bfloat16

SLOTS = 3
LEVELS = 32700.0


def momentum_list():
    ratio_now = 1.0
    ratios = [ratio_now]
    for iteration in range(KSTART + ITERS + 3):
        ratio_now = (1.0 + math.sqrt(1.0 + 4.0 * ratio_now * ratio_now)) / 2.0
        ratios.append(ratio_now)
    return [
        (ratios[KSTART - 1 + iteration] - 1.0) / ratios[KSTART + iteration]
        for iteration in range(ITERS + 1)
    ]


def signs(length):
    index = np.arange(length)
    both = index[:, None] & index[None]
    parity = np.zeros_like(both)
    while both.any():
        parity ^= both & 1
        both >>= 1
    return np.where(parity == 1, -1.0, 1.0)


def dot(a, b):
    return jnp.dot(a, b, preferred_element_type=f32)


def split_dot(matrix, values):
    upper = values.astype(bf16)
    lower = (values - upper.astype(f32)).astype(bf16)
    return dot(matrix, upper) + dot(matrix, lower)


def call(body, outs, args, prefetch=(), scratch=(), flops=0, limit=28, far=(), far_outs=False, anchors=()):
    vmem = pl.BlockSpec(memory_space=pltpu.VMEM)
    hbm = pl.BlockSpec(memory_space=pltpu.HBM)
    ahead = [pl.BlockSpec(memory_space=pl.ANY)] * len(anchors)
    size = sum(math.prod(a.shape) * a.dtype.itemsize for a in (*args, *outs, *far))
    return pl.pallas_call(
        body,
        out_shape=tuple(outs),
        in_specs=[pl.BlockSpec(memory_space=pltpu.SMEM)] * len(prefetch) + ahead + [vmem] * len(args) + [hbm] * len(far),
        out_specs=tuple([hbm if far_outs else vmem] * len(outs)),
        scratch_shapes=list(scratch),
        compiler_params=pltpu.CompilerParams(vmem_limit_bytes=limit * 2**20),
        cost_estimate=pl.CostEstimate(flops=flops, bytes_accessed=size, transcendentals=0),
    )(*prefetch, *anchors, *args, *far)


def shape(dims, dtype):
    return jax.ShapeDtypeStruct(tuple(dims), dtype)


def encode(ref, values):
    rows, depth, tile = values.shape
    flat = jnp.concatenate([values[r] for r in range(rows)], axis=0)
    bound = jnp.max(jnp.max(jnp.abs(flat), axis=0, keepdims=True), axis=1, keepdims=True)
    exponent = jnp.floor(jnp.log2(jnp.maximum(bound, 1e-30))) + 1.0
    coded = jnp.clip(jnp.round(flat * (LEVELS * jnp.exp2(-exponent))), -32767.0, 32767.0)
    ref[pl.ds(0, rows * depth)] = coded.astype(jnp.int32).astype(jnp.int16)
    ref[pl.ds(rows * depth, 16)] = jnp.broadcast_to(exponent, (16, tile)).astype(jnp.int32).astype(jnp.int16)


def decode(ref, size):
    coded = ref[pl.ds(0, size + 16)].astype(jnp.int32).astype(f32)
    return coded[:size] * (jnp.exp2(coded[size : size + 1, 0:1]) * (1.0 / LEVELS))


def decode_wide(refs, rows, depth):
    pieces = [decode(ref, rows * depth) for ref in refs]
    return jnp.concatenate(
        [jnp.concatenate([p[r * depth : (r + 1) * depth] for r in range(rows)], axis=1) for p in pieces],
        axis=0,
    )


def lateral_kernel(rows, frames, mask_ref, *refs):
    outs, held, sems = refs[5:8], refs[8:13], refs[13]
    copies = [pltpu.make_async_copy(a, b, sems.at[i]) for i, (a, b) in enumerate(zip(refs[:5], held))]
    for copy in copies:
        copy.start()
    id_ref, lo_ref, live_ref, measured_ref, masks_ref = held
    odd = lax.axis_index("lat") % 2 == 1
    own_ref = outs[0]
    depth = id_ref.shape[3]
    for ref in outs:
        ref[rows + 1] = jnp.full(ref.shape[1:], -1.0, f32)
    for copy in copies:
        copy.wait()
    for f in range(frames):
        first = lo_ref[f]
        end = first + live_ref[f]
        ids = [jnp.where((o - 1 >= first) & (o - 1 < end), id_ref[f, o], -1).astype(f32) for o in range(3)]
        for ref, row in zip(outs, (ids[1], jnp.where(odd, ids[0], ids[2]), jnp.where(odd, ids[2], ids[0]))):
            ref[rows + 1, pl.ds(f, 1), pl.ds(0, depth)] = row
        own_ref[rows, pl.ds(f, 1)] = masks_ref[pl.ds(mask_ref[f], 1)]
        for r in range(rows):
            own_ref[r, pl.ds(f, 1)] = measured_ref[f, pl.ds(r, 1)]
    for ref in outs[1:]:
        ref[pl.ds(0, rows + 1)] = own_ref[pl.ds(0, rows + 1)]


def prepare_kernel(count, rows, momentum, est_ref, prev_ref, own_ref, *refs):
    refs[2 * count][...] = own_ref[...]
    me = lax.axis_index("dep")
    for slot in range(count):
        group = pl.ds((me ^ slot) * rows, rows)
        est = est_ref[group]
        encode(refs[slot], est + momentum * (est - prev_ref[group]))
        encode(refs[count + slot], est)


def pack_ids(ids, height):
    if ids.shape[0] > height:
        half = ids.shape[1] // 2
        ids = jnp.concatenate([ids[:height, :half], ids[height:, :half]], axis=1)
    return ids.astype(jnp.int32).astype(jnp.int16)


def unpack_ids(packed, block, depth):
    ids = packed.astype(jnp.int32).astype(f32)
    if ids.shape[0] < block:
        half = ids.shape[1] // 2
        ids = jnp.concatenate([ids[:, :half], ids[:, half:]], axis=0)
    return ids[:block, :depth]


def fill_kernel(count, rows, frames, own_ref, a_ref, b_ref, *refs):
    ids_ref = refs[2 * count]
    place, last = lax.axis_index("lat"), lax.axis_size("lat") - 1
    ids_ref[...] = jnp.full(ids_ref.shape, -1.0, f32)
    ids_ref[pl.ds(0, frames)] = own_ref[rows + 1]
    ids_ref[pl.ds(frames, frames)] = a_ref[rows + 1]
    ids_ref[pl.ds(2 * frames, frames)] = jnp.where((place == 0) | (place == last), -1.0, b_ref[rows + 1])
    ids = pack_ids(ids_ref[...], refs[count].shape[0] - refs[0].shape[0])
    for coded, out in zip(refs[:count], refs[count : 2 * count]):
        size = coded.shape[0]
        out[pl.ds(0, size)] = coded[...]
        out[pl.ds(size, ids.shape[0])] = ids


def table_kernel(anchor_ref, table_ref, out_ref):
    out_ref[...] = table_ref[...]


def state_kernel(rows, tile, fresh_ref, *refs):
    put_slots(fresh_ref[...], refs, rows, tile)


def choose_t_kernel(block, prints, spread_ref, number_ref, ids_ref, choose_ref):
    tall = ids_ref[...].T.astype(bf16)
    step = 5 * 128
    width = prints * block
    for start in range(0, width, step):
        stop = min(start + step, width)
        lanes = dot(tall, spread_ref[:, start:stop])
        choose_ref[:, start:stop] = jnp.where(lanes == number_ref[0:1, start:stop], 1.0, 0.0).astype(bf16)


def project(rows, block, frames, prints, lifted, choose_ref, table_ref, acc_ref, outs):
    per = 8 if prints % 8 == 0 else 2
    tile = table_ref.shape[1]
    total = jnp.zeros((rows * block, tile), f32)
    for start in range(0, prints, per):
        summed = dot(choose_ref[pl.ds(start * block, per * block)], lifted)
        for pair in range(per // 2):
            base = 2 * pair * block
            left = jnp.concatenate(
                [
                    jnp.concatenate(
                        [
                            summed[base + k * block : base + (k + 1) * block, r * tile : (r + 1) * tile]
                            for k in (0, 1)
                        ],
                        axis=1,
                    )
                    for r in range(rows)
                ],
                axis=0,
            )
            weights = table_ref[pl.ds(start + 2 * pair, 2)].reshape(2 * tile, tile)
            total = total + dot(left.astype(bf16), weights)
    acc_ref[...] = total
    to_a_ref, to_b_ref, part_a_ref, part_b_ref = outs
    for r in range(rows):
        own, part_a, part_b = (acc_ref[pl.ds(r * block + slot * frames, frames)] for slot in range(SLOTS))
        to_a_ref[r] = own
        to_a_ref[rows + r] = part_a
        part_a_ref[r] = part_a
        to_b_ref[r] = own
        to_b_ref[rows + r] = part_b
        part_b_ref[r] = part_b


def project_kernel(count, rows, block, frames, prints, depth, *refs):
    currents, table_ref, outs = refs[:count], refs[count], refs[count + 1 : count + 5]
    choose_ref, ids_ref, acc_ref = refs[count + 5 :]
    top = rows * depth + 16
    rest = currents[0].shape[0] - top
    wide = jnp.concatenate(
        [unpack_ids(c[pl.ds(top, rest)], block, depth) for c in currents], axis=1
    )
    ids_ref[...] = wide
    for pair in range(prints // 2):
        both = jnp.concatenate(
            [jnp.where(wide == float(2 * pair + k), 1.0, 0.0).astype(f32) for k in (0, 1)], axis=0
        )
        choose_ref[pl.ds(pair * 2 * block, 2 * block)] = both.astype(bf16)
    lifted = decode_wide(currents, rows, depth).astype(bf16)
    project(rows, block, frames, prints, lifted, choose_ref, table_ref, acc_ref, outs)


def back_kernel(
    skip, rows, block, frames, prints, *refs
):
    own_ref, a_ref, b_ref, to_a_ref, part_b_ref, from_a_ref, from_b_ref, past_a_ref, past_b_ref = refs[skip : skip + 9]
    choose_ref, table_ref, grad_ref, sums_ref, left_ref, upper_ref, lower_ref = refs[skip + 9 :]
    tile = table_ref.shape[1]
    left_ref[...] = jnp.zeros_like(left_ref)
    misfit = jnp.zeros((1, tile), f32)
    for r in range(rows):
        projected = (
            to_a_ref[r] + (from_a_ref[rows + r] + from_b_ref[rows + r]),
            from_a_ref[r] + (to_a_ref[rows + r] + past_a_ref[r]),
            from_b_ref[r] + (part_b_ref[r] + past_b_ref[r]),
        )
        for slot, ref in enumerate((own_ref, a_ref, b_ref)):
            mask = ref[rows]
            residual = mask * projected[slot] - ref[r]
            if slot == 0:
                misfit = misfit + jnp.sum(residual * residual, axis=0, keepdims=True)
            weighted = (mask * residual).astype(bf16).astype(f32)
            left_ref[pl.ds(r * block + slot * frames, frames)] = weighted
    left = left_ref[...].astype(bf16)
    per = 8 if prints % 8 == 0 else 2
    for start in range(0, prints, per):
        weights = table_ref[pl.ds(start, per)].reshape(per * tile, tile)
        spread = lax.dot_general(left, weights, (((1,), (1,)), ((), ())), preferred_element_type=f32)
        for pair in range(per // 2):
            both = jnp.concatenate(
                [
                    jnp.concatenate(
                        [
                            spread[r * block : (r + 1) * block, k * tile : (k + 1) * tile]
                            for r in range(rows)
                        ],
                        axis=1,
                    )
                    for k in (2 * pair, 2 * pair + 1)
                ],
                axis=0,
            )
            upper = both.astype(bf16)
            where = pl.ds((start + 2 * pair) * block, 2 * block)
            upper_ref[where] = upper
            lower_ref[where] = (both - upper.astype(f32)).astype(bf16)
    choose = choose_ref[...]
    gradient = dot(choose, upper_ref[...]) + dot(choose, lower_ref[...])
    grad_ref[...] = gradient
    grad_sum = jnp.sum(jnp.sum(gradient * gradient, axis=0, keepdims=True), axis=1, keepdims=True)
    misfit_sum = jnp.sum(misfit, axis=1, keepdims=True)
    lane = lax.broadcasted_iota(jnp.int32, sums_ref.shape, 1)
    sums_ref[...] = jnp.where(lane < sums_ref.shape[1] // 2, misfit_sum, grad_sum)


def shrink(scale, sums_ref, current, grad, had_ref, limits_ref):
    total = jnp.sum(sums_ref[...], axis=0, keepdims=True)
    half = total.shape[1] // 2
    step = 0.5 * total[:, 0:1] / (total[:, half : half + 1] + tiny_eps)
    moved = current - step * grad
    coefficients = split_dot(had_ref[...], moved) * scale
    limit = step * limits_ref[...]
    limit = jnp.concatenate([limit] * (moved.shape[1] // limit.shape[1]), axis=1)
    clipped = jnp.clip(coefficients, -limit, limit)
    return moved - split_dot(had_ref[...], clipped) * scale


def first_kernel(count, rows, block, frames, prints, depth, scale, momentum, *refs):
    currents, refs = refs[:count], refs[count:]
    states, refs = refs[:count], refs[count:]
    sums_ref, grad_ref, had_ref, limits_ref, choose_ref, table_ref = refs[:6]
    outs, refs = refs[6:10], refs[10:]
    current_ref, fresh_ref, acc_ref = refs

    current, state = decode_wide(currents, rows, depth), decode_wide(states, rows, depth)
    fresh = shrink(scale, sums_ref, current, grad_ref[...], had_ref, limits_ref)
    fresh_ref[...] = fresh
    current = fresh + momentum * (fresh - state)
    current_ref[...] = current
    project(rows, block, frames, prints, current.astype(bf16), choose_ref, table_ref, acc_ref, outs)


def put_slots(fresh, refs, rows, tile):
    depth = fresh.shape[0] // len(refs)
    for slot in [*range(1, len(refs)), 0]:
        piece = fresh[slot * depth : (slot + 1) * depth]
        encode(refs[slot], jnp.stack([piece[:, r * tile : (r + 1) * tile] for r in range(rows)]))


def last_kernel(count, rows, scale, sums_ref, current_ref, grad_ref, had_ref, limits_ref, *fresh_refs):
    tile = limits_ref.shape[1]
    fresh = shrink(scale, sums_ref, current_ref[...], grad_ref[...], had_ref, limits_ref)
    put_slots(fresh, fresh_refs, rows, tile)


def finish_kernel(count, rows, momentum, *refs):
    states, fresh = refs[:count], refs[count : 2 * count]
    refined_hbm, ahead_hbm, refined_ref, ahead_ref, sems = refs[2 * count :]
    me = lax.axis_index("dep")
    copies = []
    for slot in range(count):
        group = pl.ds((me ^ slot) * rows, rows)
        size = math.prod(refined_ref.shape[1:3])
        now, before = decode(fresh[slot], size), decode(states[slot], size)
        refined_ref[slot] = now.reshape(refined_ref.shape[1:])
        ahead_ref[slot] = (now + momentum * (now - before)).reshape(ahead_ref.shape[1:])
        copies.append(pltpu.make_async_copy(refined_ref.at[slot], refined_hbm.at[group], sems.at[0, slot]))
        copies.append(pltpu.make_async_copy(ahead_ref.at[slot], ahead_hbm.at[group], sems.at[1, slot]))
        copies[-2].start()
        copies[-1].start()
    for copy in copies:
        copy.wait()


def depth_exchange(parts):
    count = len(parts)
    return [parts[0]] + [
        lax.ppermute(parts[s], "dep", [(i, i ^ s) for i in range(count)]) for s in range(1, count)
    ]


def partner_exchange(to_a, to_b):
    count = lax.axis_size("lat")
    pairs_a = [(i, i ^ 1) for i in range(count)]
    pairs_b = [(i, (i + 1 if i % 2 else i - 1) % count) for i in range(count)]
    return lax.ppermute(to_a, "lat", pairs_a), lax.ppermute(to_b, "lat", pairs_b)


def past_exchange(part_a, part_b):
    count = lax.axis_size("lat")
    past_a = [(i, (i + 2 if i % 2 else i - 2) % count) for i in range(count)]
    past_b = [(i, (i - 2 if i % 2 else i + 2) % count) for i in range(count)]
    return lax.ppermute(part_b, "lat", past_a), lax.ppermute(part_a, "lat", past_b)


def local(
    estimate,
    previous,
    measured,
    foot_table,
    foot_id,
    foot_lo,
    foot_count,
    mask_table,
    mask_id,
    thresholds,
):
    row_total, depth_local, tile = estimate.shape
    count = lax.axis_size("dep")
    lat_count = lax.axis_size("lat")
    rows = row_total // count
    depth = depth_local * count
    frames = measured.shape[1]
    prints = foot_table.shape[0]
    block = -(-SLOTS * frames // 8) * 8
    width = rows * tile
    momenta = momentum_list()
    scale = float(0.7071067811865476 ** (depth.bit_length() - 1))
    had = jnp.asarray(signs(depth), bf16)
    limits = jnp.broadcast_to(thresholds[:, None], (depth, tile))
    volume = (rows, depth_local, tile)
    coded = shape((rows * depth_local + 16, tile), jnp.int16)

    small = [
        jnp.transpose(foot_id, (1, 3, 0, 2)),
        jnp.transpose(foot_lo, (1, 0, 2)),
        jnp.transpose(foot_count, (1, 0, 2)),
        jnp.transpose(measured, (1, 0, 2)),
        mask_table,
    ]
    pack = shape((rows + 2, frames, tile), f32)
    own, to_a, to_b = call(
        functools.partial(lateral_kernel, rows, frames),
        [pack] * 3,
        [],
        far=small,
        scratch=[*(pltpu.VMEM(a.shape, a.dtype) for a in small), pltpu.SemaphoreType.DMA((len(small),))],
        prefetch=[mask_id[:, 0]],
        limit=56,
    )
    packs = [own, *partner_exchange(to_a, to_b)]

    fold = 2 if 2 * depth_local <= tile else 1
    more = -(-block // (16 * fold)) * 16
    prepared = call(
        functools.partial(prepare_kernel, count, rows, momenta[0]), [coded] * (2 * count) + [pack], [estimate, previous, own]
    )
    packs[0] = prepared[-1]
    currents = call(
        functools.partial(fill_kernel, count, rows, frames),
        [shape((rows * depth_local + 16 + more, tile), jnp.int16)] * count,
        [*packs, *prepared[:count]],
        scratch=[pltpu.VMEM((fold * more, tile), f32)],
    )
    (table,) = call(
        table_kernel,
        [shape(foot_table.shape, foot_table.dtype)],
        [foot_table],
        anchors=currents[:1],
    )
    currents = depth_exchange(currents)
    states = depth_exchange(prepared[count : 2 * count])
    lanes = np.arange(prints * block)
    spread = jnp.asarray(lanes[None] % block == np.arange(block)[:, None], bf16)
    number = jnp.asarray(np.broadcast_to(lanes // block, (8, prints * block)), f32)
    sizes = (rows, block, frames, prints)
    acc = pltpu.VMEM((rows * block, tile), f32)
    part, double = shape((rows, frames, tile), f32), shape((2 * rows, frames, tile), f32)
    work = 2 * prints * block * width * (depth + tile)
    *parts, choose, ids = call(
        functools.partial(project_kernel, count, *sizes, depth_local),
        [double, double, part, part, shape((prints * block, depth), bf16), shape((block, depth), f32)],
        [*currents, table],
        scratch=[acc],
        flops=work,
    )
    (choose_t,) = call(
        functools.partial(choose_t_kernel, block, prints),
        [shape((depth, prints * block), bf16)],
        [spread, number, ids],
    )

    def step_sums(parts, hidden):
        to_a, to_b, part_a, part_b = parts
        gradient, sums = call(
            functools.partial(back_kernel, len(hidden), *sizes),
            [shape((depth, width), f32), shape((count * lat_count, tile), f32)],
            [
                *packs,
                to_a,
                part_b,
                *partner_exchange(to_a, to_b),
                *past_exchange(part_a, part_b),
                choose_t,
                table,
            ],
            scratch=[
                pltpu.VMEM((rows * block, tile), f32),
                pltpu.VMEM((prints * block, width), bf16),
                pltpu.VMEM((prints * block, width), bf16),
            ],
            flops=2 * work,
            anchors=hidden,
        )
        return gradient, lax.all_to_all(sums, ("lat", "dep"), split_axis=0, concat_axis=0, tiled=True)

    gradient, sums = step_sums(parts, states[1:])
    done = call(
        functools.partial(first_kernel, count, *sizes, depth_local, scale, momenta[1]),
        [double, double, part, part] + [shape((depth, width), f32)] * 2,
        [*currents, *states, sums, gradient, had, limits, choose, table],
        scratch=[acc],
        flops=work,
    )
    parts, current = done[:4], done[4]
    states = depth_exchange(
        call(functools.partial(state_kernel, rows, tile), [coded] * count, [done[5]])
    )
    gradient, sums = step_sums(parts, [])
    fresh = depth_exchange(
        call(
            functools.partial(last_kernel, count, rows, scale),
            [coded] * count,
            [sums, current, gradient, had, limits],
        )
    )
    return call(
        functools.partial(finish_kernel, count, rows, momenta[2]),
        [shape(estimate.shape, f32)] * 2,
        [*states, *fresh],
        far_outs=True,
        scratch=[
            pltpu.VMEM((count, *volume), f32),
            pltpu.VMEM((count, *volume), f32),
            pltpu.SemaphoreType.DMA((2, count)),
        ],
    )


def solution(mesh):
    in_specs = (
        P(None, "dep", "lat"),
        P(None, "dep", "lat"),
        P("dep", None, "lat"),
        P(),
        P("lat", None, "dep", None),
        P("lat", None, "dep"),
        P("lat", None, "dep"),
        P(),
        P(None, "lat"),
        P(),
    )
    out_specs = (P(None, "dep", "lat"), P(None, "dep", "lat"))
    return jax.shard_map(local, mesh=mesh, in_specs=in_specs, out_specs=out_specs, check_vma=False)
```

```python
import functools
import math

import jax
import jax.numpy as jnp
import numpy as np
from jax import lax
from jax.experimental import pallas as pl
from jax.experimental.pallas import tpu as pltpu
from jax.sharding import PartitionSpec as P

ITERS = 2
KSTART = 8

tiny_eps = 1e-06
f32 = jnp.float32
bf16 = jnp.bfloat16

SLOTS = 3
LEVELS = 32700.0


def momentum_list():
    ratio_now = 1.0
    ratios = [ratio_now]
    for iteration in range(KSTART + ITERS + 3):
        ratio_now = (1.0 + math.sqrt(1.0 + 4.0 * ratio_now * ratio_now)) / 2.0
        ratios.append(ratio_now)
    return [
        (ratios[KSTART - 1 + iteration] - 1.0) / ratios[KSTART + iteration]
        for iteration in range(ITERS + 1)
    ]


def signs(length):
    index = np.arange(length)
    both = index[:, None] & index[None]
    parity = np.zeros_like(both)
    while both.any():
        parity ^= both & 1
        both >>= 1
    return np.where(parity == 1, -1.0, 1.0)


def dot(a, b):
    return jnp.dot(a, b, preferred_element_type=f32)


def split_dot(matrix, values):
    upper = values.astype(bf16)
    lower = (values - upper.astype(f32)).astype(bf16)
    return dot(matrix, upper) + dot(matrix, lower)


def call(body, outs, args, prefetch=(), scratch=(), flops=0, limit=28, far=(), far_outs=False, anchors=()):
    vmem = pl.BlockSpec(memory_space=pltpu.VMEM)
    hbm = pl.BlockSpec(memory_space=pltpu.HBM)
    ahead = [pl.BlockSpec(memory_space=pl.ANY)] * len(anchors)
    size = sum(math.prod(a.shape) * a.dtype.itemsize for a in (*args, *outs, *far))
    return pl.pallas_call(
        body,
        out_shape=tuple(outs),
        in_specs=[pl.BlockSpec(memory_space=pltpu.SMEM)] * len(prefetch) + ahead + [vmem] * len(args) + [hbm] * len(far),
        out_specs=tuple([hbm if far_outs else vmem] * len(outs)),
        scratch_shapes=list(scratch),
        compiler_params=pltpu.CompilerParams(vmem_limit_bytes=limit * 2**20),
        cost_estimate=pl.CostEstimate(flops=flops, bytes_accessed=size, transcendentals=0),
    )(*prefetch, *anchors, *args, *(pltpu.with_memory_space_constraint(a, pltpu.HBM) for a in far))


def shape(dims, dtype):
    return jax.ShapeDtypeStruct(tuple(dims), dtype)


def encode(ref, values):
    rows, depth, tile = values.shape
    flat = jnp.concatenate([values[r] for r in range(rows)], axis=0)
    bound = jnp.max(jnp.max(jnp.abs(flat), axis=0, keepdims=True), axis=1, keepdims=True)
    exponent = jnp.floor(jnp.log2(jnp.maximum(bound, 1e-30))) + 1.0
    coded = jnp.clip(jnp.round(flat * (LEVELS * jnp.exp2(-exponent))), -32767.0, 32767.0)
    ref[pl.ds(0, rows * depth)] = coded.astype(jnp.int32).astype(jnp.int16)
    ref[pl.ds(rows * depth, 16)] = jnp.broadcast_to(exponent, (16, tile)).astype(jnp.int32).astype(jnp.int16)


def decode(ref, size):
    coded = ref[pl.ds(0, size + 16)].astype(jnp.int32).astype(f32)
    return coded[:size] * (jnp.exp2(coded[size : size + 1, 0:1]) * (1.0 / LEVELS))


def decode_wide(refs, rows, depth):
    pieces = [decode(ref, rows * depth) for ref in refs]
    return jnp.concatenate(
        [jnp.concatenate([p[r * depth : (r + 1) * depth] for r in range(rows)], axis=1) for p in pieces],
        axis=0,
    )


def lateral_kernel(rows, frames, *refs):
    volumes, kept = refs[6:8], refs[11:13]
    outs, held, sems, volume_sems = refs[8:11], refs[13:19], refs[19], refs[20]
    copies = [pltpu.make_async_copy(a, b, sems.at[i]) for i, (a, b) in enumerate(zip(refs[:6], held))]
    cuts = volume_sems.shape[1]
    groups = [pl.ds(i * (kept[0].shape[0] // cuts), kept[0].shape[0] // cuts) for i in range(cuts)]
    brought = [
        pltpu.make_async_copy(a.at[group], b.at[group], volume_sems.at[j, i])
        for j, (a, b) in enumerate(zip(volumes, kept))
        for i, group in enumerate(groups)
    ]
    for copy in (*copies, *brought):
        copy.start()
    mask_ref, id_ref, lo_ref, live_ref, measured_ref, masks_ref = held
    odd = lax.axis_index("lat") % 2 == 1
    own_ref = outs[0]
    depth = id_ref.shape[3]
    for ref in outs:
        ref[rows + 1] = jnp.full(ref.shape[1:], -1.0, f32)
    for copy in copies:
        copy.wait()
    for f in range(frames):
        first = lo_ref[f]
        end = first + live_ref[f]
        ids = [jnp.where((o - 1 >= first) & (o - 1 < end), id_ref[f, o], -1).astype(f32) for o in range(3)]
        for ref, row in zip(outs, (ids[1], jnp.where(odd, ids[0], ids[2]), jnp.where(odd, ids[2], ids[0]))):
            ref[rows + 1, pl.ds(f, 1), pl.ds(0, depth)] = row
        own_ref[rows, pl.ds(f, 1)] = masks_ref[pl.ds(mask_ref[0, f], 1)]
        for r in range(rows):
            own_ref[r, pl.ds(f, 1)] = measured_ref[f, pl.ds(r, 1)]
    for ref in outs[1:]:
        ref[pl.ds(0, rows + 1)] = own_ref[pl.ds(0, rows + 1)]
    for copy in brought:
        copy.wait()


def prepare_kernel(count, rows, momentum, est_ref, prev_ref, *refs):
    me = lax.axis_index("dep")
    for slot in range(count):
        group = pl.ds((me ^ slot) * rows, rows)
        est = est_ref[group]
        encode(refs[slot], est + momentum * (est - prev_ref[group]))
        encode(refs[count + slot], est)


def pack_ids(ids, height):
    if ids.shape[0] > height:
        half = ids.shape[1] // 2
        ids = jnp.concatenate([ids[:height, :half], ids[height:, :half]], axis=1)
    return ids.astype(jnp.int32).astype(jnp.int16)


def unpack_ids(packed, block, depth):
    ids = packed.astype(jnp.int32).astype(f32)
    if ids.shape[0] < block:
        half = ids.shape[1] // 2
        ids = jnp.concatenate([ids[:, :half], ids[:, half:]], axis=0)
    return ids[:block, :depth]


def fill_kernel(count, rows, frames, own_ref, a_ref, b_ref, *refs):
    ids_ref = refs[2 * count]
    place, last = lax.axis_index("lat"), lax.axis_size("lat") - 1
    ids_ref[...] = jnp.full(ids_ref.shape, -1.0, f32)
    ids_ref[pl.ds(0, frames)] = own_ref[rows + 1]
    ids_ref[pl.ds(frames, frames)] = a_ref[rows + 1]
    ids_ref[pl.ds(2 * frames, frames)] = jnp.where((place == 0) | (place == last), -1.0, b_ref[rows + 1])
    ids = pack_ids(ids_ref[...], refs[count].shape[0] - refs[0].shape[0])
    for coded, out in zip(refs[:count], refs[count : 2 * count]):
        size = coded.shape[0]
        out[pl.ds(0, size)] = coded[...]
        out[pl.ds(size, ids.shape[0])] = ids


def table_kernel(anchor_ref, table_ref, out_ref):
    out_ref[...] = table_ref[...]


def state_kernel(rows, tile, fresh_ref, *refs):
    put_slots(fresh_ref[...], refs, rows, tile)


def choose_t_kernel(block, prints, spread_ref, number_ref, ids_ref, choose_ref):
    tall = ids_ref[...].T.astype(bf16)
    step = 5 * 128
    width = prints * block
    for start in range(0, width, step):
        stop = min(start + step, width)
        lanes = dot(tall, spread_ref[:, start:stop])
        choose_ref[:, start:stop] = jnp.where(lanes == number_ref[0:1, start:stop], 1.0, 0.0).astype(bf16)


def project(rows, block, frames, prints, lifted, choose_ref, table_ref, acc_ref, outs):
    per = 8 if prints % 8 == 0 else 2
    tile = table_ref.shape[1]
    total = jnp.zeros((rows * block, tile), f32)
    for start in range(0, prints, per):
        summed = dot(choose_ref[pl.ds(start * block, per * block)], lifted)
        for pair in range(per // 2):
            base = 2 * pair * block
            left = jnp.concatenate(
                [
                    jnp.concatenate(
                        [
                            summed[base + k * block : base + (k + 1) * block, r * tile : (r + 1) * tile]
                            for k in (0, 1)
                        ],
                        axis=1,
                    )
                    for r in range(rows)
                ],
                axis=0,
            )
            weights = table_ref[pl.ds(start + 2 * pair, 2)].reshape(2 * tile, tile)
            total = total + dot(left.astype(bf16), weights)
    acc_ref[...] = total
    to_a_ref, to_b_ref, part_a_ref, part_b_ref = outs
    for r in range(rows):
        own, part_a, part_b = (acc_ref[pl.ds(r * block + slot * frames, frames)] for slot in range(SLOTS))
        to_a_ref[r] = own
        to_a_ref[rows + r] = part_a
        part_a_ref[r] = part_a
        to_b_ref[r] = own
        to_b_ref[rows + r] = part_b
        part_b_ref[r] = part_b


def project_kernel(count, rows, block, frames, prints, depth, *refs):
    currents, table_ref, outs = refs[:count], refs[count], refs[count + 1 : count + 5]
    choose_ref, ids_ref, acc_ref = refs[count + 5 :]
    top = rows * depth + 16
    rest = currents[0].shape[0] - top
    wide = jnp.concatenate(
        [unpack_ids(c[pl.ds(top, rest)], block, depth) for c in currents], axis=1
    )
    ids_ref[...] = wide
    for pair in range(prints // 2):
        both = jnp.concatenate(
            [jnp.where(wide == float(2 * pair + k), 1.0, 0.0).astype(f32) for k in (0, 1)], axis=0
        )
        choose_ref[pl.ds(pair * 2 * block, 2 * block)] = both.astype(bf16)
    lifted = decode_wide(currents, rows, depth).astype(bf16)
    project(rows, block, frames, prints, lifted, choose_ref, table_ref, acc_ref, outs)


def back_kernel(
    skip, rows, block, frames, prints, *refs
):
    own_ref, a_ref, b_ref, to_a_ref, part_b_ref, from_a_ref, from_b_ref, past_a_ref, past_b_ref = refs[skip : skip + 9]
    choose_ref, table_ref, grad_ref, sums_ref, left_ref, upper_ref, lower_ref = refs[skip + 9 :]
    tile = table_ref.shape[1]
    left_ref[...] = jnp.zeros_like(left_ref)
    misfit = jnp.zeros((1, tile), f32)
    for r in range(rows):
        projected = (
            to_a_ref[r] + (from_a_ref[rows + r] + from_b_ref[rows + r]),
            from_a_ref[r] + (to_a_ref[rows + r] + past_a_ref[r]),
            from_b_ref[r] + (part_b_ref[r] + past_b_ref[r]),
        )
        for slot, ref in enumerate((own_ref, a_ref, b_ref)):
            mask = ref[rows]
            residual = mask * projected[slot] - ref[r]
            if slot == 0:
                misfit = misfit + jnp.sum(residual * residual, axis=0, keepdims=True)
            weighted = (mask * residual).astype(bf16).astype(f32)
            left_ref[pl.ds(r * block + slot * frames, frames)] = weighted
    left = left_ref[...].astype(bf16)
    per = 8 if prints % 8 == 0 else 2
    for start in range(0, prints, per):
        weights = table_ref[pl.ds(start, per)].reshape(per * tile, tile)
        spread = lax.dot_general(left, weights, (((1,), (1,)), ((), ())), preferred_element_type=f32)
        for pair in range(per // 2):
            both = jnp.concatenate(
                [
                    jnp.concatenate(
                        [
                            spread[r * block : (r + 1) * block, k * tile : (k + 1) * tile]
                            for r in range(rows)
                        ],
                        axis=1,
                    )
                    for k in (2 * pair, 2 * pair + 1)
                ],
                axis=0,
            )
            upper = both.astype(bf16)
            where = pl.ds((start + 2 * pair) * block, 2 * block)
            upper_ref[where] = upper
            lower_ref[where] = (both - upper.astype(f32)).astype(bf16)
    choose = choose_ref[...]
    gradient = dot(choose, upper_ref[...]) + dot(choose, lower_ref[...])
    grad_ref[...] = gradient
    grad_sum = jnp.sum(jnp.sum(gradient * gradient, axis=0, keepdims=True), axis=1, keepdims=True)
    misfit_sum = jnp.sum(misfit, axis=1, keepdims=True)
    lane = lax.broadcasted_iota(jnp.int32, sums_ref.shape, 1)
    sums_ref[...] = jnp.where(lane < sums_ref.shape[1] // 2, misfit_sum, grad_sum)


def shrink(scale, sums_ref, current, grad, had_ref, limits_ref):
    total = jnp.sum(sums_ref[...], axis=0, keepdims=True)
    half = total.shape[1] // 2
    step = 0.5 * total[:, 0:1] / (total[:, half : half + 1] + tiny_eps)
    moved = current - step * grad
    coefficients = split_dot(had_ref[...], moved) * scale
    limit = step * limits_ref[...]
    limit = jnp.concatenate([limit] * (moved.shape[1] // limit.shape[1]), axis=1)
    clipped = jnp.clip(coefficients, -limit, limit)
    return moved - split_dot(had_ref[...], clipped) * scale


def first_kernel(count, rows, block, frames, prints, depth, scale, momentum, *refs):
    currents, refs = refs[:count], refs[count:]
    states, refs = refs[:count], refs[count:]
    sums_ref, grad_ref, had_ref, limits_ref, choose_ref, table_ref = refs[:6]
    outs, refs = refs[6:10], refs[10:]
    current_ref, fresh_ref, acc_ref = refs

    current, state = decode_wide(currents, rows, depth), decode_wide(states, rows, depth)
    fresh = shrink(scale, sums_ref, current, grad_ref[...], had_ref, limits_ref)
    fresh_ref[...] = fresh
    current = fresh + momentum * (fresh - state)
    current_ref[...] = current
    project(rows, block, frames, prints, current.astype(bf16), choose_ref, table_ref, acc_ref, outs)


def put_slots(fresh, refs, rows, tile):
    depth = fresh.shape[0] // len(refs)
    for slot in [*range(1, len(refs)), 0]:
        piece = fresh[slot * depth : (slot + 1) * depth]
        encode(refs[slot], jnp.stack([piece[:, r * tile : (r + 1) * tile] for r in range(rows)]))


def last_kernel(count, rows, scale, sums_ref, current_ref, grad_ref, had_ref, limits_ref, *fresh_refs):
    tile = limits_ref.shape[1]
    fresh = shrink(scale, sums_ref, current_ref[...], grad_ref[...], had_ref, limits_ref)
    put_slots(fresh, fresh_refs, rows, tile)


def finish_kernel(count, rows, momentum, *refs):
    states, fresh = refs[:count], refs[count : 2 * count]
    refined_hbm, ahead_hbm, refined_ref, ahead_ref, sems = refs[2 * count :]
    me = lax.axis_index("dep")
    copies = []
    for slot in range(count):
        group = pl.ds((me ^ slot) * rows, rows)
        size = math.prod(refined_ref.shape[1:3])
        now, before = decode(fresh[slot], size), decode(states[slot], size)
        refined_ref[slot] = now.reshape(refined_ref.shape[1:])
        ahead_ref[slot] = (now + momentum * (now - before)).reshape(ahead_ref.shape[1:])
        copies.append(pltpu.make_async_copy(refined_ref.at[slot], refined_hbm.at[group], sems.at[0, slot]))
        copies.append(pltpu.make_async_copy(ahead_ref.at[slot], ahead_hbm.at[group], sems.at[1, slot]))
        copies[-2].start()
        copies[-1].start()
    for copy in copies:
        copy.wait()


def depth_exchange(parts):
    count = len(parts)
    moved = {s: lax.ppermute(parts[s], "dep", [(i, i ^ s) for i in range(count)]) for s in range(count - 1, 0, -1)}
    return [parts[0]] + [moved[s] for s in range(1, count)]


def partner_exchange(to_a, to_b):
    count = lax.axis_size("lat")
    pairs_a = [(i, i ^ 1) for i in range(count)]
    pairs_b = [(i, (i + 1 if i % 2 else i - 1) % count) for i in range(count)]
    return lax.ppermute(to_a, "lat", pairs_a), lax.ppermute(to_b, "lat", pairs_b)


def past_exchange(part_a, part_b):
    count = lax.axis_size("lat")
    past_a = [(i, (i + 2 if i % 2 else i - 2) % count) for i in range(count)]
    past_b = [(i, (i - 2 if i % 2 else i + 2) % count) for i in range(count)]
    return lax.ppermute(part_b, "lat", past_a), lax.ppermute(part_a, "lat", past_b)


def local(
    estimate,
    previous,
    measured,
    foot_table,
    foot_id,
    foot_lo,
    foot_count,
    mask_table,
    mask_id,
    thresholds,
):
    row_total, depth_local, tile = estimate.shape
    count = lax.axis_size("dep")
    lat_count = lax.axis_size("lat")
    rows = row_total // count
    depth = depth_local * count
    frames = measured.shape[1]
    prints = foot_table.shape[0]
    block = -(-SLOTS * frames // 8) * 8
    width = rows * tile
    momenta = momentum_list()
    scale = float(0.7071067811865476 ** (depth.bit_length() - 1))
    had = jnp.asarray(signs(depth), bf16)
    limits = jnp.broadcast_to(thresholds[:, None], (depth, tile))
    volume = (rows, depth_local, tile)
    coded = shape((rows * depth_local + 16, tile), jnp.int16)

    small = [
        mask_id.T,
        jnp.transpose(foot_id, (1, 3, 0, 2)),
        jnp.transpose(foot_lo, (1, 0, 2)),
        jnp.transpose(foot_count, (1, 0, 2)),
        jnp.transpose(measured, (1, 0, 2)),
        mask_table,
    ]
    pack = shape((rows + 2, frames, tile), f32)
    own, to_a, to_b, near_estimate, near_previous = call(
        functools.partial(lateral_kernel, rows, frames),
        [pack] * 3 + [shape(estimate.shape, f32)] * 2,
        [],
        far=[*small, estimate, previous],
        scratch=[
            pltpu.SMEM(small[0].shape, jnp.int32),
            *(pltpu.VMEM(a.shape, a.dtype) for a in small[1:]),
            pltpu.SemaphoreType.DMA((len(small),)),
            pltpu.SemaphoreType.DMA((2, count)),
        ],

    )
    packs = [own, *partner_exchange(to_a, to_b)]

    fold = 2 if 2 * depth_local <= tile else 1
    more = -(-block // (16 * fold)) * 16
    prepared = call(
        functools.partial(prepare_kernel, count, rows, momenta[0]), [coded] * (2 * count), [near_estimate, near_previous]
    )
    currents = call(
        functools.partial(fill_kernel, count, rows, frames),
        [shape((rows * depth_local + 16 + more, tile), jnp.int16)] * count,
        [*packs, *prepared[:count]],
        scratch=[pltpu.VMEM((fold * more, tile), f32)],
    )
    (table,) = call(
        table_kernel,
        [shape(foot_table.shape, foot_table.dtype)],
        [foot_table],
        anchors=currents[:1],
    )
    currents = depth_exchange(currents)
    states = depth_exchange(prepared[count : 2 * count])
    lanes = np.arange(prints * block)
    spread = jnp.asarray(lanes[None] % block == np.arange(block)[:, None], bf16)
    number = jnp.asarray(np.broadcast_to(lanes // block, (8, prints * block)), f32)
    sizes = (rows, block, frames, prints)
    acc = pltpu.VMEM((rows * block, tile), f32)
    part, double = shape((rows, frames, tile), f32), shape((2 * rows, frames, tile), f32)
    work = 2 * prints * block * width * (depth + tile)
    *parts, choose, ids = call(
        functools.partial(project_kernel, count, *sizes, depth_local),
        [double, double, part, part, shape((prints * block, depth), bf16), shape((block, depth), f32)],
        [*currents, table],
        scratch=[acc],
        flops=work,
    )
    (choose_t,) = call(
        functools.partial(choose_t_kernel, block, prints),
        [shape((depth, prints * block), bf16)],
        [spread, number, ids],
    )

    def step_sums(parts, hidden):
        to_a, to_b, part_a, part_b = parts
        gradient, sums = call(
            functools.partial(back_kernel, len(hidden), *sizes),
            [shape((depth, width), f32), shape((count * lat_count, tile), f32)],
            [
                *packs,
                to_a,
                part_b,
                *partner_exchange(to_a, to_b),
                *past_exchange(part_a, part_b),
                choose_t,
                table,
            ],
            scratch=[
                pltpu.VMEM((rows * block, tile), f32),
                pltpu.VMEM((prints * block, width), bf16),
                pltpu.VMEM((prints * block, width), bf16),
            ],
            flops=2 * work,
            anchors=hidden,
        )
        return gradient, lax.all_to_all(sums, ("lat", "dep"), split_axis=0, concat_axis=0, tiled=True)

    gradient, sums = step_sums(parts, states[1:])
    done = call(
        functools.partial(first_kernel, count, *sizes, depth_local, scale, momenta[1]),
        [double, double, part, part] + [shape((depth, width), f32)] * 2,
        [*currents, *states, sums, gradient, had, limits, choose, table],
        scratch=[acc],
        flops=work,
    )
    parts, current = done[:4], done[4]
    states = depth_exchange(
        call(functools.partial(state_kernel, rows, tile), [coded] * count, [done[5]])
    )
    gradient, sums = step_sums(parts, [])
    fresh = depth_exchange(
        call(
            functools.partial(last_kernel, count, rows, scale),
            [coded] * count,
            [sums, current, gradient, had, limits],
        )
    )
    return call(
        functools.partial(finish_kernel, count, rows, momenta[2]),
        [shape(estimate.shape, f32)] * 2,
        [*states, *fresh],
        far_outs=True,
        scratch=[
            pltpu.VMEM((count, *volume), f32),
            pltpu.VMEM((count, *volume), f32),
            pltpu.SemaphoreType.DMA((2, count)),
        ],
    )


def solution(mesh):
    in_specs = (
        P(None, "dep", "lat"),
        P(None, "dep", "lat"),
        P("dep", None, "lat"),
        P(),
        P("lat", None, "dep", None),
        P("lat", None, "dep"),
        P("lat", None, "dep"),
        P(),
        P(None, "lat"),
        P(),
    )
    out_specs = (P(None, "dep", "lat"), P(None, "dep", "lat"))
    return jax.shard_map(local, mesh=mesh, in_specs=in_specs, out_specs=out_specs, check_vma=False)
```

```python
import functools
import math

import jax
import jax.numpy as jnp
import numpy as np
from jax import lax
from jax.experimental import pallas as pl
from jax.experimental.pallas import tpu as pltpu
from jax.sharding import PartitionSpec as P

ITERS = 2
KSTART = 8

tiny_eps = 1e-06
f32 = jnp.float32
bf16 = jnp.bfloat16

SLOTS = 3
LEVELS = 32700.0


def momentum_list():
    ratio_now = 1.0
    ratios = [ratio_now]
    for iteration in range(KSTART + ITERS + 3):
        ratio_now = (1.0 + math.sqrt(1.0 + 4.0 * ratio_now * ratio_now)) / 2.0
        ratios.append(ratio_now)
    return [
        (ratios[KSTART - 1 + iteration] - 1.0) / ratios[KSTART + iteration]
        for iteration in range(ITERS + 1)
    ]


def signs(length):
    index = np.arange(length)
    both = index[:, None] & index[None]
    parity = np.zeros_like(both)
    while both.any():
        parity ^= both & 1
        both >>= 1
    return np.where(parity == 1, -1.0, 1.0)


def dot(a, b):
    return jnp.dot(a, b, preferred_element_type=f32)


def split_dot(matrix, values):
    upper = values.astype(bf16)
    lower = (values - upper.astype(f32)).astype(bf16)
    return dot(matrix, upper) + dot(matrix, lower)


def call(body, outs, args, prefetch=(), scratch=(), flops=0, limit=28, far=(), far_outs=False, anchors=()):
    vmem = pl.BlockSpec(memory_space=pltpu.VMEM)
    hbm = pl.BlockSpec(memory_space=pltpu.HBM)
    ahead = [pl.BlockSpec(memory_space=pl.ANY)] * len(anchors)
    size = sum(math.prod(a.shape) * a.dtype.itemsize for a in (*args, *outs, *far))
    return pl.pallas_call(
        body,
        out_shape=tuple(outs),
        in_specs=[pl.BlockSpec(memory_space=pltpu.SMEM)] * len(prefetch) + ahead + [vmem] * len(args) + [hbm] * len(far),
        out_specs=tuple([hbm if far_outs else vmem] * len(outs)),
        scratch_shapes=list(scratch),
        compiler_params=pltpu.CompilerParams(vmem_limit_bytes=limit * 2**20),
        cost_estimate=pl.CostEstimate(flops=flops, bytes_accessed=size, transcendentals=0),
    )(*prefetch, *anchors, *args, *(pltpu.with_memory_space_constraint(a, pltpu.HBM) for a in far))


def shape(dims, dtype):
    return jax.ShapeDtypeStruct(tuple(dims), dtype)


def encode(ref, values):
    rows, depth, tile = values.shape
    flat = jnp.concatenate([values[r] for r in range(rows)], axis=0)
    bound = jnp.max(jnp.max(jnp.abs(flat), axis=0, keepdims=True), axis=1, keepdims=True)
    exponent = jnp.floor(jnp.log2(jnp.maximum(bound, 1e-30))) + 1.0
    coded = jnp.clip(jnp.round(flat * (LEVELS * jnp.exp2(-exponent))), -32767.0, 32767.0)
    ref[pl.ds(0, rows * depth)] = coded.astype(jnp.int32).astype(jnp.int16)
    ref[pl.ds(rows * depth, 16)] = jnp.broadcast_to(exponent, (16, tile)).astype(jnp.int32).astype(jnp.int16)


def decode(ref, size):
    coded = ref[pl.ds(0, size + 16)].astype(jnp.int32).astype(f32)
    return coded[:size] * (jnp.exp2(coded[size : size + 1, 0:1]) * (1.0 / LEVELS))


def decode_wide(refs, rows, depth):
    pieces = [decode(ref, rows * depth) for ref in refs]
    return jnp.concatenate(
        [jnp.concatenate([p[r * depth : (r + 1) * depth] for r in range(rows)], axis=1) for p in pieces],
        axis=0,
    )


def lateral_kernel(rows, frames, *refs):
    volumes, kept = refs[6:8], refs[11:13]
    outs, held, sems, volume_sems = refs[8:11], refs[13:19], refs[19], refs[20]
    copies = [pltpu.make_async_copy(a, b, sems.at[i]) for i, (a, b) in enumerate(zip(refs[:6], held))]
    cuts = volume_sems.shape[1]
    groups = [pl.ds(i * (kept[0].shape[0] // cuts), kept[0].shape[0] // cuts) for i in range(cuts)]
    brought = [
        pltpu.make_async_copy(a.at[group], b.at[group], volume_sems.at[j, i])
        for j, (a, b) in enumerate(zip(volumes, kept))
        for i, group in enumerate(groups)
    ]
    for copy in (*copies, *brought):
        copy.start()
    mask_ref, id_ref, lo_ref, live_ref, measured_ref, masks_ref = held
    odd = lax.axis_index("lat") % 2 == 1
    own_ref = outs[0]
    depth = id_ref.shape[3]
    for ref in outs:
        ref[rows + 1] = jnp.full(ref.shape[1:], -1.0, f32)
    for copy in copies:
        copy.wait()
    for f in range(frames):
        first = lo_ref[f]
        end = first + live_ref[f]
        ids = [jnp.where((o - 1 >= first) & (o - 1 < end), id_ref[f, o], -1).astype(f32) for o in range(3)]
        for ref, row in zip(outs, (ids[1], jnp.where(odd, ids[0], ids[2]), jnp.where(odd, ids[2], ids[0]))):
            ref[rows + 1, pl.ds(f, 1), pl.ds(0, depth)] = row
        own_ref[rows, pl.ds(f, 1)] = masks_ref[pl.ds(mask_ref[0, f], 1)]
        for r in range(rows):
            own_ref[r, pl.ds(f, 1)] = measured_ref[f, pl.ds(r, 1)]
    for ref in outs[1:]:
        ref[pl.ds(0, rows + 1)] = own_ref[pl.ds(0, rows + 1)]
    for copy in brought:
        copy.wait()


def prepare_kernel(count, rows, momentum, est_ref, prev_ref, *refs):
    me = lax.axis_index("dep")
    for slot in range(count):
        group = pl.ds((me ^ slot) * rows, rows)
        est = est_ref[group]
        encode(refs[slot], est + momentum * (est - prev_ref[group]))
        if slot < len(refs) - count:
            encode(refs[count + slot], est)


def pack_ids(ids, height):
    if ids.shape[0] > height:
        half = ids.shape[1] // 2
        ids = jnp.concatenate([ids[:height, :half], ids[height:, :half]], axis=1)
    return ids.astype(jnp.int32).astype(jnp.int16)


def unpack_ids(packed, block, depth):
    ids = packed.astype(jnp.int32).astype(f32)
    if ids.shape[0] < block:
        half = ids.shape[1] // 2
        ids = jnp.concatenate([ids[:, :half], ids[:, half:]], axis=0)
    return ids[:block, :depth]


def estimate_kernel(early, count, rows, anchor_ref, est_ref, *refs):
    me = lax.axis_index("dep")
    for slot in range(early, count):
        encode(refs[slot - early], est_ref[pl.ds((me ^ slot) * rows, rows)])


def fill_kernel(count, rows, frames, own_ref, a_ref, b_ref, *refs):
    ids_ref = refs[2 * count]
    place, last = lax.axis_index("lat"), lax.axis_size("lat") - 1
    ids_ref[...] = jnp.full(ids_ref.shape, -1.0, f32)
    ids_ref[pl.ds(0, frames)] = own_ref[rows + 1]
    ids_ref[pl.ds(frames, frames)] = a_ref[rows + 1]
    ids_ref[pl.ds(2 * frames, frames)] = jnp.where((place == 0) | (place == last), -1.0, b_ref[rows + 1])
    ids = pack_ids(ids_ref[...], refs[count].shape[0] - refs[0].shape[0])
    for coded, out in zip(refs[:count], refs[count : 2 * count]):
        size = coded.shape[0]
        out[pl.ds(0, size)] = coded[...]
        out[pl.ds(size, ids.shape[0])] = ids


def table_kernel(anchor_ref, table_ref, out_ref):
    out_ref[...] = table_ref[...]


def pass_kernel(*refs):
    refs[-1][...] = refs[-2][...]


def state_kernel(rows, tile, fresh_ref, *refs):
    put_slots(fresh_ref[...], refs, rows, tile)


def choose_t_kernel(block, prints, spread_ref, number_ref, ids_ref, choose_ref):
    tall = ids_ref[...].T.astype(bf16)
    step = 5 * 128
    width = prints * block
    for start in range(0, width, step):
        stop = min(start + step, width)
        lanes = dot(tall, spread_ref[:, start:stop])
        choose_ref[:, start:stop] = jnp.where(lanes == number_ref[0:1, start:stop], 1.0, 0.0).astype(bf16)


def project(rows, block, frames, prints, lifted, choose_ref, table_ref, acc_ref, outs):
    per = 8 if prints % 8 == 0 else 2
    tile = table_ref.shape[1]
    total = jnp.zeros((rows * block, tile), f32)
    for start in range(0, prints, per):
        summed = dot(choose_ref[pl.ds(start * block, per * block)], lifted)
        for pair in range(per // 2):
            base = 2 * pair * block
            left = jnp.concatenate(
                [
                    jnp.concatenate(
                        [
                            summed[base + k * block : base + (k + 1) * block, r * tile : (r + 1) * tile]
                            for k in (0, 1)
                        ],
                        axis=1,
                    )
                    for r in range(rows)
                ],
                axis=0,
            )
            weights = table_ref[pl.ds(start + 2 * pair, 2)].reshape(2 * tile, tile)
            total = total + dot(left.astype(bf16), weights)
    acc_ref[...] = total
    to_a_ref, to_b_ref, part_a_ref, part_b_ref = outs
    for r in range(rows):
        own, part_a, part_b = (acc_ref[pl.ds(r * block + slot * frames, frames)] for slot in range(SLOTS))
        to_a_ref[r] = own
        to_a_ref[rows + r] = part_a
        part_a_ref[r] = part_a
        to_b_ref[r] = own
        to_b_ref[rows + r] = part_b
        part_b_ref[r] = part_b


def project_kernel(count, rows, block, frames, prints, depth, *refs):
    currents, table_ref, outs = refs[:count], refs[count], refs[count + 1 : count + 5]
    choose_ref, ids_ref, acc_ref = refs[count + 5 :]
    top = rows * depth + 16
    rest = currents[0].shape[0] - top
    wide = jnp.concatenate(
        [unpack_ids(c[pl.ds(top, rest)], block, depth) for c in currents], axis=1
    )
    ids_ref[...] = wide
    for pair in range(prints // 2):
        both = jnp.concatenate(
            [jnp.where(wide == float(2 * pair + k), 1.0, 0.0).astype(f32) for k in (0, 1)], axis=0
        )
        choose_ref[pl.ds(pair * 2 * block, 2 * block)] = both.astype(bf16)
    lifted = decode_wide(currents, rows, depth).astype(bf16)
    project(rows, block, frames, prints, lifted, choose_ref, table_ref, acc_ref, outs)


def back_kernel(
    skip, rows, block, frames, prints, *refs
):
    own_ref, a_ref, b_ref, to_a_ref, part_b_ref, from_a_ref, from_b_ref, past_a_ref, past_b_ref = refs[skip : skip + 9]
    choose_ref, table_ref, grad_ref, sums_ref, left_ref, upper_ref, lower_ref = refs[skip + 9 :]
    tile = table_ref.shape[1]
    left_ref[...] = jnp.zeros_like(left_ref)
    misfit = jnp.zeros((1, tile), f32)
    for r in range(rows):
        projected = (
            to_a_ref[r] + (from_a_ref[rows + r] + from_b_ref[rows + r]),
            from_a_ref[r] + (to_a_ref[rows + r] + past_a_ref[r]),
            from_b_ref[r] + (part_b_ref[r] + past_b_ref[r]),
        )
        for slot, ref in enumerate((own_ref, a_ref, b_ref)):
            mask = ref[rows]
            residual = mask * projected[slot] - ref[r]
            if slot == 0:
                misfit = misfit + jnp.sum(residual * residual, axis=0, keepdims=True)
            weighted = (mask * residual).astype(bf16).astype(f32)
            left_ref[pl.ds(r * block + slot * frames, frames)] = weighted
    left = left_ref[...].astype(bf16)
    per = 8 if prints % 8 == 0 else 2
    for start in range(0, prints, per):
        weights = table_ref[pl.ds(start, per)].reshape(per * tile, tile)
        spread = lax.dot_general(left, weights, (((1,), (1,)), ((), ())), preferred_element_type=f32)
        for pair in range(per // 2):
            both = jnp.concatenate(
                [
                    jnp.concatenate(
                        [
                            spread[r * block : (r + 1) * block, k * tile : (k + 1) * tile]
                            for r in range(rows)
                        ],
                        axis=1,
                    )
                    for k in (2 * pair, 2 * pair + 1)
                ],
                axis=0,
            )
            upper = both.astype(bf16)
            where = pl.ds((start + 2 * pair) * block, 2 * block)
            upper_ref[where] = upper
            lower_ref[where] = (both - upper.astype(f32)).astype(bf16)
    choose = choose_ref[...]
    gradient = dot(choose, upper_ref[...]) + dot(choose, lower_ref[...])
    grad_ref[...] = gradient
    grad_sum = jnp.sum(jnp.sum(gradient * gradient, axis=0, keepdims=True), axis=1, keepdims=True)
    misfit_sum = jnp.sum(misfit, axis=1, keepdims=True)
    lane = lax.broadcasted_iota(jnp.int32, sums_ref.shape, 1)
    sums_ref[...] = jnp.where(lane < sums_ref.shape[1] // 2, misfit_sum, grad_sum)


def shrink(scale, sums_ref, current, grad, had_ref, limits_ref):
    total = jnp.sum(sums_ref[...], axis=0, keepdims=True)
    half = total.shape[1] // 2
    step = 0.5 * total[:, 0:1] / (total[:, half : half + 1] + tiny_eps)
    moved = current - step * grad
    coefficients = split_dot(had_ref[...], moved) * scale
    limit = step * limits_ref[...]
    limit = jnp.concatenate([limit] * (moved.shape[1] // limit.shape[1]), axis=1)
    clipped = jnp.clip(coefficients, -limit, limit)
    return moved - split_dot(had_ref[...], clipped) * scale


def first_kernel(count, rows, block, frames, prints, depth, scale, momentum, *refs):
    currents, refs = refs[:count], refs[count:]
    states, refs = refs[:count], refs[count:]
    sums_ref, grad_ref, had_ref, limits_ref, choose_ref, table_ref = refs[:6]
    outs, refs = refs[6:10], refs[10:]
    current_ref, fresh_ref, acc_ref = refs

    current, state = decode_wide(currents, rows, depth), decode_wide(states, rows, depth)
    fresh = shrink(scale, sums_ref, current, grad_ref[...], had_ref, limits_ref)
    fresh_ref[...] = fresh
    current = fresh + momentum * (fresh - state)
    current_ref[...] = current
    project(rows, block, frames, prints, current.astype(bf16), choose_ref, table_ref, acc_ref, outs)


def put_slots(fresh, refs, rows, tile):
    depth = fresh.shape[0] // len(refs)
    for slot in [*range(1, len(refs)), 0]:
        piece = fresh[slot * depth : (slot + 1) * depth]
        encode(refs[slot], jnp.stack([piece[:, r * tile : (r + 1) * tile] for r in range(rows)]))


def last_kernel(count, rows, scale, sums_ref, current_ref, grad_ref, had_ref, limits_ref, *fresh_refs):
    tile = limits_ref.shape[1]
    fresh = shrink(scale, sums_ref, current_ref[...], grad_ref[...], had_ref, limits_ref)
    put_slots(fresh, fresh_refs, rows, tile)


def finish_kernel(count, rows, momentum, *refs):
    states, fresh = refs[:count], refs[count : 2 * count]
    refined_hbm, ahead_hbm, refined_ref, ahead_ref, sems = refs[2 * count :]
    me = lax.axis_index("dep")
    copies = []
    for slot in range(count):
        group = pl.ds((me ^ slot) * rows, rows)
        size = math.prod(refined_ref.shape[1:3])
        now, before = decode(fresh[slot], size), decode(states[slot], size)
        refined_ref[slot] = now.reshape(refined_ref.shape[1:])
        ahead_ref[slot] = (now + momentum * (now - before)).reshape(ahead_ref.shape[1:])
        copies.append(pltpu.make_async_copy(refined_ref.at[slot], refined_hbm.at[group], sems.at[0, slot]))
        copies.append(pltpu.make_async_copy(ahead_ref.at[slot], ahead_hbm.at[group], sems.at[1, slot]))
        copies[-2].start()
        copies[-1].start()
    for copy in copies:
        copy.wait()


def depth_exchange(parts):
    count = len(parts)
    moved = {s: lax.ppermute(parts[s], "dep", [(i, i ^ s) for i in range(count)]) for s in range(count - 1, 0, -1)}
    return [parts[0]] + [moved[s] for s in range(1, count)]


def partner_exchange(to_a, to_b):
    count = lax.axis_size("lat")
    pairs_a = [(i, i ^ 1) for i in range(count)]
    pairs_b = [(i, (i + 1 if i % 2 else i - 1) % count) for i in range(count)]
    return lax.ppermute(to_a, "lat", pairs_a), lax.ppermute(to_b, "lat", pairs_b)


def past_exchange(part_a, part_b):
    count = lax.axis_size("lat")
    past_a = [(i, (i + 2 if i % 2 else i - 2) % count) for i in range(count)]
    past_b = [(i, (i - 2 if i % 2 else i + 2) % count) for i in range(count)]
    return lax.ppermute(part_b, "lat", past_a), lax.ppermute(part_a, "lat", past_b)


def local(
    estimate,
    previous,
    measured,
    foot_table,
    foot_id,
    foot_lo,
    foot_count,
    mask_table,
    mask_id,
    thresholds,
):
    row_total, depth_local, tile = estimate.shape
    count = lax.axis_size("dep")
    lat_count = lax.axis_size("lat")
    rows = row_total // count
    depth = depth_local * count
    frames = measured.shape[1]
    prints = foot_table.shape[0]
    block = -(-SLOTS * frames // 8) * 8
    width = rows * tile
    momenta = momentum_list()
    scale = float(0.7071067811865476 ** (depth.bit_length() - 1))
    had = jnp.asarray(signs(depth), bf16)
    limits = jnp.broadcast_to(thresholds[:, None], (depth, tile))
    volume = (rows, depth_local, tile)
    coded = shape((rows * depth_local + 16, tile), jnp.int16)

    small = [
        mask_id.T,
        jnp.transpose(foot_id, (1, 3, 0, 2)),
        jnp.transpose(foot_lo, (1, 0, 2)),
        jnp.transpose(foot_count, (1, 0, 2)),
        jnp.transpose(measured, (1, 0, 2)),
        mask_table,
    ]
    pack = shape((rows + 2, frames, tile), f32)
    own, to_a, to_b, near_estimate, near_previous = call(
        functools.partial(lateral_kernel, rows, frames),
        [pack] * 3 + [shape(estimate.shape, f32)] * 2,
        [],
        far=[*small, estimate, previous],
        scratch=[
            pltpu.SMEM(small[0].shape, jnp.int32),
            *(pltpu.VMEM(a.shape, a.dtype) for a in small[1:]),
            pltpu.SemaphoreType.DMA((len(small),)),
            pltpu.SemaphoreType.DMA((2, count)),
        ],

    )
    packs = [own, *partner_exchange(to_a, to_b)]

    fold = 2 if 2 * depth_local <= tile else 1
    more = -(-block // (16 * fold)) * 16
    early = max(1, count - 1)
    prepared = call(
        functools.partial(prepare_kernel, count, rows, momenta[0]), [coded] * (count + early), [near_estimate, near_previous]
    )
    currents = call(
        functools.partial(fill_kernel, count, rows, frames),
        [shape((rows * depth_local + 16 + more, tile), jnp.int16)] * count,
        [*packs, *prepared[:count]],
        scratch=[pltpu.VMEM((fold * more, tile), f32)],
    )
    (table,) = call(
        table_kernel,
        [shape(foot_table.shape, foot_table.dtype)],
        [foot_table],
        anchors=currents[:1],
    )
    currents = depth_exchange(currents)
    lanes = np.arange(prints * block)
    spread = jnp.asarray(lanes[None] % block == np.arange(block)[:, None], bf16)
    number = jnp.asarray(np.broadcast_to(lanes // block, (8, prints * block)), f32)
    sizes = (rows, block, frames, prints)
    acc = pltpu.VMEM((rows * block, tile), f32)
    part, double = shape((rows, frames, tile), f32), shape((2 * rows, frames, tile), f32)
    work = 2 * prints * block * width * (depth + tile)
    *parts, choose, ids = call(
        functools.partial(project_kernel, count, *sizes, depth_local),
        [double, double, part, part, shape((prints * block, depth), bf16), shape((block, depth), f32)],
        [*currents, table],
        scratch=[acc],
        flops=work,
    )
    (choose_t,) = call(
        functools.partial(choose_t_kernel, block, prints),
        [shape((depth, prints * block), bf16)],
        [spread, number, ids],
    )

    def exchange_parts(parts):
        return [*partner_exchange(*parts[:2]), *past_exchange(*parts[2:])]

    def step_sums(parts, received, hidden, late):
        to_a, part_b = parts[0], parts[3]
        gradient, sums = call(
            functools.partial(back_kernel, len(hidden), *sizes),
            [shape((depth, width), f32), shape((count * lat_count, tile), f32)],
            [
                *packs,
                to_a,
                part_b,
                *received,
                choose_t,
                table,
            ],
            scratch=[
                pltpu.VMEM((rows * block, tile), f32),
                pltpu.VMEM((prints * block, width), bf16),
                pltpu.VMEM((prints * block, width), bf16),
            ],
            flops=2 * work,
            anchors=hidden,
        )
        if late:
            (sums,) = call(pass_kernel, [shape(sums.shape, f32)], [sums], anchors=late)
        return gradient, lax.all_to_all(sums, ("lat", "dep"), split_axis=0, concat_axis=0, tiled=True)

    received = exchange_parts(parts)
    later = call(
        functools.partial(estimate_kernel, early, count, rows),
        [coded] * (count - early),
        [near_estimate],
        anchors=[received[0]],
    )
    states = depth_exchange([*prepared[count:], *later])
    gradient, sums = step_sums(parts, received, list(states[1:early]), states[early:])
    done = call(
        functools.partial(first_kernel, count, *sizes, depth_local, scale, momenta[1]),
        [double, double, part, part] + [shape((depth, width), f32)] * 2,
        [*currents, *states, sums, gradient, had, limits, choose, table],
        scratch=[acc],
        flops=work,
    )
    parts, current = done[:4], done[4]
    states = depth_exchange(
        call(functools.partial(state_kernel, rows, tile), [coded] * count, [done[5]])
    )
    gradient, sums = step_sums(parts, exchange_parts(parts), [], [])
    fresh = depth_exchange(
        call(
            functools.partial(last_kernel, count, rows, scale),
            [coded] * count,
            [sums, current, gradient, had, limits],
        )
    )
    return call(
        functools.partial(finish_kernel, count, rows, momenta[2]),
        [shape(estimate.shape, f32)] * 2,
        [*states, *fresh],
        far_outs=True,
        scratch=[
            pltpu.VMEM((count, *volume), f32),
            pltpu.VMEM((count, *volume), f32),
            pltpu.SemaphoreType.DMA((2, count)),
        ],
    )


def solution(mesh):
    in_specs = (
        P(None, "dep", "lat"),
        P(None, "dep", "lat"),
        P("dep", None, "lat"),
        P(),
        P("lat", None, "dep", None),
        P("lat", None, "dep"),
        P("lat", None, "dep"),
        P(),
        P(None, "lat"),
        P(),
    )
    out_specs = (P(None, "dep", "lat"), P(None, "dep", "lat"))
    return jax.shard_map(local, mesh=mesh, in_specs=in_specs, out_specs=out_specs, check_vma=False)
```

```python
import functools
import math

import jax
import jax.numpy as jnp
import numpy as np
from jax import lax
from jax.experimental import pallas as pl
from jax.experimental.pallas import tpu as pltpu
from jax.sharding import PartitionSpec as P

ITERS = 2
KSTART = 8

tiny_eps = 1e-06
f32 = jnp.float32
bf16 = jnp.bfloat16

SLOTS = 3
LEVELS = 32700.0


def momentum_list():
    ratio_now = 1.0
    ratios = [ratio_now]
    for iteration in range(KSTART + ITERS + 3):
        ratio_now = (1.0 + math.sqrt(1.0 + 4.0 * ratio_now * ratio_now)) / 2.0
        ratios.append(ratio_now)
    return [
        (ratios[KSTART - 1 + iteration] - 1.0) / ratios[KSTART + iteration]
        for iteration in range(ITERS + 1)
    ]


def signs(length):
    index = np.arange(length)
    both = index[:, None] & index[None]
    parity = np.zeros_like(both)
    while both.any():
        parity ^= both & 1
        both >>= 1
    return np.where(parity == 1, -1.0, 1.0)


def dot(a, b):
    return jnp.dot(a, b, preferred_element_type=f32)


def split_dot(matrix, values):
    upper = values.astype(bf16)
    lower = (values - upper.astype(f32)).astype(bf16)
    return dot(matrix, upper) + dot(matrix, lower)


def call(body, outs, args, prefetch=(), scratch=(), flops=0, limit=28, far=(), far_outs=False, anchors=()):
    vmem = pl.BlockSpec(memory_space=pltpu.VMEM)
    hbm = pl.BlockSpec(memory_space=pltpu.HBM)
    ahead = [pl.BlockSpec(memory_space=pl.ANY)] * len(anchors)
    size = sum(math.prod(a.shape) * a.dtype.itemsize for a in (*args, *outs, *far))
    return pl.pallas_call(
        body,
        out_shape=tuple(outs),
        in_specs=[pl.BlockSpec(memory_space=pltpu.SMEM)] * len(prefetch) + ahead + [vmem] * len(args) + [hbm] * len(far),
        out_specs=tuple([hbm if far_outs else vmem] * len(outs)),
        scratch_shapes=list(scratch),
        compiler_params=pltpu.CompilerParams(vmem_limit_bytes=limit * 2**20),
        cost_estimate=pl.CostEstimate(flops=flops, bytes_accessed=size, transcendentals=0),
    )(*prefetch, *anchors, *args, *(pltpu.with_memory_space_constraint(a, pltpu.HBM) for a in far))


def shape(dims, dtype):
    return jax.ShapeDtypeStruct(tuple(dims), dtype)


def encode(ref, values):
    rows, depth, tile = values.shape
    flat = jnp.concatenate([values[r] for r in range(rows)], axis=0)
    bound = jnp.max(jnp.max(jnp.abs(flat), axis=0, keepdims=True), axis=1, keepdims=True)
    exponent = jnp.floor(jnp.log2(jnp.maximum(bound, 1e-30))) + 1.0
    coded = jnp.clip(jnp.round(flat * (LEVELS * jnp.exp2(-exponent))), -32767.0, 32767.0)
    ref[pl.ds(0, rows * depth)] = coded.astype(jnp.int32).astype(jnp.int16)
    ref[pl.ds(rows * depth, 16)] = jnp.broadcast_to(exponent, (16, tile)).astype(jnp.int32).astype(jnp.int16)


def decode(ref, size):
    coded = ref[pl.ds(0, size + 16)].astype(jnp.int32).astype(f32)
    return coded[:size] * (jnp.exp2(coded[size : size + 1, 0:1]) * (1.0 / LEVELS))


def decode_wide(refs, rows, depth):
    pieces = [decode(ref, rows * depth) for ref in refs]
    return jnp.concatenate(
        [jnp.concatenate([p[r * depth : (r + 1) * depth] for r in range(rows)], axis=1) for p in pieces],
        axis=0,
    )


def lateral_kernel(rows, frames, *refs):
    volumes, kept = refs[6:8], refs[11:13]
    outs, held, sems, volume_sems = refs[8:11], refs[13:19], refs[19], refs[20]
    copies = [pltpu.make_async_copy(a, b, sems.at[i]) for i, (a, b) in enumerate(zip(refs[:6], held))]
    cuts = volume_sems.shape[1]
    groups = [pl.ds(i * (kept[0].shape[0] // cuts), kept[0].shape[0] // cuts) for i in range(cuts)]
    brought = [
        pltpu.make_async_copy(a.at[group], b.at[group], volume_sems.at[j, i])
        for j, (a, b) in enumerate(zip(volumes, kept))
        for i, group in enumerate(groups)
    ]
    for copy in (*copies, *brought):
        copy.start()
    mask_ref, id_ref, lo_ref, live_ref, measured_ref, masks_ref = held
    odd = lax.axis_index("lat") % 2 == 1
    own_ref = outs[0]
    depth = id_ref.shape[3]
    for ref in outs:
        ref[rows + 1] = jnp.full(ref.shape[1:], -1.0, f32)
    for copy in copies:
        copy.wait()
    for f in range(frames):
        first = lo_ref[f]
        end = first + live_ref[f]
        ids = [jnp.where((o - 1 >= first) & (o - 1 < end), id_ref[f, o], -1).astype(f32) for o in range(3)]
        for ref, row in zip(outs, (ids[1], jnp.where(odd, ids[0], ids[2]), jnp.where(odd, ids[2], ids[0]))):
            ref[rows + 1, pl.ds(f, 1), pl.ds(0, depth)] = row
        own_ref[rows, pl.ds(f, 1)] = masks_ref[pl.ds(mask_ref[0, f], 1)]
        for r in range(rows):
            own_ref[r, pl.ds(f, 1)] = measured_ref[f, pl.ds(r, 1)]
    for ref in outs[1:]:
        ref[pl.ds(0, rows + 1)] = own_ref[pl.ds(0, rows + 1)]
    for copy in brought:
        copy.wait()


def prepare_kernel(count, rows, momentum, est_ref, prev_ref, *refs):
    me = lax.axis_index("dep")
    for slot in range(count):
        group = pl.ds((me ^ slot) * rows, rows)
        est = est_ref[group]
        encode(refs[slot], est + momentum * (est - prev_ref[group]))
        if slot < len(refs) - count:
            encode(refs[count + slot], est)


def pack_ids(ids, height):
    if ids.shape[0] > height:
        half = ids.shape[1] // 2
        ids = jnp.concatenate([ids[:height, :half], ids[height:, :half]], axis=1)
    return ids.astype(jnp.int32).astype(jnp.int16)


def unpack_ids(packed, block, depth):
    ids = packed.astype(jnp.int32).astype(f32)
    if ids.shape[0] < block:
        half = ids.shape[1] // 2
        ids = jnp.concatenate([ids[:, :half], ids[:, half:]], axis=0)
    return ids[:block, :depth]


def estimate_kernel(early, count, rows, anchor_ref, est_ref, *refs):
    me = lax.axis_index("dep")
    for slot in range(early, count):
        encode(refs[slot - early], est_ref[pl.ds((me ^ slot) * rows, rows)])


def fill_kernel(count, rows, frames, own_ref, a_ref, b_ref, *refs):
    ids_ref = refs[2 * count]
    place, last = lax.axis_index("lat"), lax.axis_size("lat") - 1
    ids_ref[...] = jnp.full(ids_ref.shape, -1.0, f32)
    ids_ref[pl.ds(0, frames)] = own_ref[rows + 1]
    ids_ref[pl.ds(frames, frames)] = a_ref[rows + 1]
    ids_ref[pl.ds(2 * frames, frames)] = jnp.where((place == 0) | (place == last), -1.0, b_ref[rows + 1])
    ids = pack_ids(ids_ref[...], refs[count].shape[0] - refs[0].shape[0])
    for coded, out in zip(refs[:count], refs[count : 2 * count]):
        size = coded.shape[0]
        out[pl.ds(0, size)] = coded[...]
        out[pl.ds(size, ids.shape[0])] = ids


def table_kernel(anchor_ref, table_ref, out_ref):
    out_ref[...] = table_ref[...]


def pass_kernel(*refs):
    refs[-1][...] = refs[-2][...]


def state_kernel(rows, tile, fresh_ref, *refs):
    put_slots(fresh_ref[...], refs, rows, tile)


def choose_t_kernel(block, prints, spread_ref, number_ref, ids_ref, choose_ref):
    tall = ids_ref[...].T.astype(bf16)
    step = 5 * 128
    width = prints * block
    for start in range(0, width, step):
        stop = min(start + step, width)
        lanes = dot(tall, spread_ref[:, start:stop])
        choose_ref[:, start:stop] = jnp.where(lanes == number_ref[0:1, start:stop], 1.0, 0.0).astype(bf16)


def project(rows, block, frames, prints, lifted, choose_ref, table_ref, acc_ref, outs):
    per = 16 if prints % 16 == 0 else 2
    tile = table_ref.shape[1]
    total = jnp.zeros((rows * block, tile), f32)
    for start in range(0, prints, per):
        summed = dot(choose_ref[pl.ds(start * block, per * block)], lifted)
        for pair in range(per // 2):
            base = 2 * pair * block
            left = jnp.concatenate(
                [
                    jnp.concatenate(
                        [
                            summed[base + k * block : base + (k + 1) * block, r * tile : (r + 1) * tile]
                            for k in (0, 1)
                        ],
                        axis=1,
                    )
                    for r in range(rows)
                ],
                axis=0,
            )
            weights = table_ref[pl.ds(start + 2 * pair, 2)].reshape(2 * tile, tile)
            total = total + dot(left.astype(bf16), weights)
    acc_ref[...] = total
    to_a_ref, to_b_ref, part_a_ref, part_b_ref = outs
    for r in range(rows):
        own, part_a, part_b = (acc_ref[pl.ds(r * block + slot * frames, frames)] for slot in range(SLOTS))
        to_a_ref[r] = own
        to_a_ref[rows + r] = part_a
        part_a_ref[r] = part_a
        to_b_ref[r] = own
        to_b_ref[rows + r] = part_b
        part_b_ref[r] = part_b


def project_kernel(count, rows, block, frames, prints, depth, *refs):
    currents, table_ref, outs = refs[:count], refs[count], refs[count + 1 : count + 5]
    choose_ref, ids_ref, acc_ref = refs[count + 5 :]
    top = rows * depth + 16
    rest = currents[0].shape[0] - top
    wide = jnp.concatenate(
        [unpack_ids(c[pl.ds(top, rest)], block, depth) for c in currents], axis=1
    )
    ids_ref[...] = wide
    for pair in range(prints // 2):
        both = jnp.concatenate(
            [jnp.where(wide == float(2 * pair + k), 1.0, 0.0).astype(f32) for k in (0, 1)], axis=0
        )
        choose_ref[pl.ds(pair * 2 * block, 2 * block)] = both.astype(bf16)
    lifted = decode_wide(currents, rows, depth).astype(bf16)
    project(rows, block, frames, prints, lifted, choose_ref, table_ref, acc_ref, outs)


def back_kernel(
    skip, rows, block, frames, prints, *refs
):
    own_ref, a_ref, b_ref, to_a_ref, part_b_ref, from_a_ref, from_b_ref, past_a_ref, past_b_ref = refs[skip : skip + 9]
    choose_ref, table_ref, grad_ref, sums_ref, left_ref, upper_ref, lower_ref = refs[skip + 9 :]
    tile = table_ref.shape[1]
    left_ref[...] = jnp.zeros_like(left_ref)
    misfit = jnp.zeros((1, tile), f32)
    for r in range(rows):
        projected = (
            to_a_ref[r] + (from_a_ref[rows + r] + from_b_ref[rows + r]),
            from_a_ref[r] + (to_a_ref[rows + r] + past_a_ref[r]),
            from_b_ref[r] + (part_b_ref[r] + past_b_ref[r]),
        )
        for slot, ref in enumerate((own_ref, a_ref, b_ref)):
            mask = ref[rows]
            residual = mask * projected[slot] - ref[r]
            if slot == 0:
                misfit = misfit + jnp.sum(residual * residual, axis=0, keepdims=True)
            weighted = (mask * residual).astype(bf16).astype(f32)
            left_ref[pl.ds(r * block + slot * frames, frames)] = weighted
    left = left_ref[...].astype(bf16)
    per = 8 if prints % 8 == 0 else 2
    for start in range(0, prints, per):
        weights = table_ref[pl.ds(start, per)].reshape(per * tile, tile)
        spread = lax.dot_general(left, weights, (((1,), (1,)), ((), ())), preferred_element_type=f32)
        for pair in range(per // 2):
            both = jnp.concatenate(
                [
                    jnp.concatenate(
                        [
                            spread[r * block : (r + 1) * block, k * tile : (k + 1) * tile]
                            for r in range(rows)
                        ],
                        axis=1,
                    )
                    for k in (2 * pair, 2 * pair + 1)
                ],
                axis=0,
            )
            upper = both.astype(bf16)
            where = pl.ds((start + 2 * pair) * block, 2 * block)
            upper_ref[where] = upper
            lower_ref[where] = (both - upper.astype(f32)).astype(bf16)
    choose = choose_ref[...]
    gradient = dot(choose, upper_ref[...]) + dot(choose, lower_ref[...])
    grad_ref[...] = gradient
    grad_sum = jnp.sum(jnp.sum(gradient * gradient, axis=0, keepdims=True), axis=1, keepdims=True)
    misfit_sum = jnp.sum(misfit, axis=1, keepdims=True)
    lane = lax.broadcasted_iota(jnp.int32, sums_ref.shape, 1)
    sums_ref[...] = jnp.where(lane < sums_ref.shape[1] // 2, misfit_sum, grad_sum)


def shrink(scale, sums_ref, current, grad, had_ref, limits_ref):
    total = jnp.sum(sums_ref[...], axis=0, keepdims=True)
    half = total.shape[1] // 2
    step = 0.5 * total[:, 0:1] / (total[:, half : half + 1] + tiny_eps)
    moved = current - step * grad
    coefficients = split_dot(had_ref[...], moved) * scale
    limit = step * limits_ref[...]
    limit = jnp.concatenate([limit] * (moved.shape[1] // limit.shape[1]), axis=1)
    clipped = jnp.clip(coefficients, -limit, limit)
    return moved - split_dot(had_ref[...], clipped) * scale


def first_kernel(count, rows, block, frames, prints, depth, scale, momentum, *refs):
    currents, refs = refs[:count], refs[count:]
    states, refs = refs[:count], refs[count:]
    sums_ref, grad_ref, had_ref, limits_ref, choose_ref, table_ref = refs[:6]
    outs, refs = refs[6:10], refs[10:]
    current_ref, fresh_ref, acc_ref = refs

    current, state = decode_wide(currents, rows, depth), decode_wide(states, rows, depth)
    fresh = shrink(scale, sums_ref, current, grad_ref[...], had_ref, limits_ref)
    fresh_ref[...] = fresh
    current = fresh + momentum * (fresh - state)
    current_ref[...] = current
    project(rows, block, frames, prints, current.astype(bf16), choose_ref, table_ref, acc_ref, outs)


def put_slots(fresh, refs, rows, tile):
    depth = fresh.shape[0] // len(refs)
    for slot in [*range(1, len(refs)), 0]:
        piece = fresh[slot * depth : (slot + 1) * depth]
        encode(refs[slot], jnp.stack([piece[:, r * tile : (r + 1) * tile] for r in range(rows)]))


def last_kernel(count, rows, scale, sums_ref, current_ref, grad_ref, had_ref, limits_ref, *fresh_refs):
    tile = limits_ref.shape[1]
    fresh = shrink(scale, sums_ref, current_ref[...], grad_ref[...], had_ref, limits_ref)
    put_slots(fresh, fresh_refs, rows, tile)


def finish_kernel(count, rows, momentum, *refs):
    states, fresh = refs[:count], refs[count : 2 * count]
    refined_hbm, ahead_hbm, refined_ref, ahead_ref, sems = refs[2 * count :]
    me = lax.axis_index("dep")
    copies = []
    for slot in range(count):
        group = pl.ds((me ^ slot) * rows, rows)
        size = math.prod(refined_ref.shape[1:3])
        now, before = decode(fresh[slot], size), decode(states[slot], size)
        refined_ref[slot] = now.reshape(refined_ref.shape[1:])
        ahead_ref[slot] = (now + momentum * (now - before)).reshape(ahead_ref.shape[1:])
        copies.append(pltpu.make_async_copy(refined_ref.at[slot], refined_hbm.at[group], sems.at[0, slot]))
        copies.append(pltpu.make_async_copy(ahead_ref.at[slot], ahead_hbm.at[group], sems.at[1, slot]))
        copies[-2].start()
        copies[-1].start()
    for copy in copies:
        copy.wait()


def depth_exchange(parts):
    count = len(parts)
    moved = {s: lax.ppermute(parts[s], "dep", [(i, i ^ s) for i in range(count)]) for s in range(count - 1, 0, -1)}
    return [parts[0]] + [moved[s] for s in range(1, count)]


def partner_exchange(to_a, to_b):
    count = lax.axis_size("lat")
    pairs_a = [(i, i ^ 1) for i in range(count)]
    pairs_b = [(i, (i + 1 if i % 2 else i - 1) % count) for i in range(count)]
    return lax.ppermute(to_a, "lat", pairs_a), lax.ppermute(to_b, "lat", pairs_b)


def past_exchange(part_a, part_b):
    count = lax.axis_size("lat")
    past_a = [(i, (i + 2 if i % 2 else i - 2) % count) for i in range(count)]
    past_b = [(i, (i - 2 if i % 2 else i + 2) % count) for i in range(count)]
    return lax.ppermute(part_b, "lat", past_a), lax.ppermute(part_a, "lat", past_b)


def local(
    estimate,
    previous,
    measured,
    foot_table,
    foot_id,
    foot_lo,
    foot_count,
    mask_table,
    mask_id,
    thresholds,
):
    row_total, depth_local, tile = estimate.shape
    count = lax.axis_size("dep")
    lat_count = lax.axis_size("lat")
    rows = row_total // count
    depth = depth_local * count
    frames = measured.shape[1]
    prints = foot_table.shape[0]
    block = -(-SLOTS * frames // 8) * 8
    width = rows * tile
    momenta = momentum_list()
    scale = float(0.7071067811865476 ** (depth.bit_length() - 1))
    had = jnp.asarray(signs(depth), bf16)
    limits = jnp.broadcast_to(thresholds[:, None], (depth, tile))
    volume = (rows, depth_local, tile)
    coded = shape((rows * depth_local + 16, tile), jnp.int16)

    small = [
        mask_id.T,
        jnp.transpose(foot_id, (1, 3, 0, 2)),
        jnp.transpose(foot_lo, (1, 0, 2)),
        jnp.transpose(foot_count, (1, 0, 2)),
        jnp.transpose(measured, (1, 0, 2)),
        mask_table,
    ]
    pack = shape((rows + 2, frames, tile), f32)
    own, to_a, to_b, near_estimate, near_previous = call(
        functools.partial(lateral_kernel, rows, frames),
        [pack] * 3 + [shape(estimate.shape, f32)] * 2,
        [],
        far=[*small, estimate, previous],
        scratch=[
            pltpu.SMEM(small[0].shape, jnp.int32),
            *(pltpu.VMEM(a.shape, a.dtype) for a in small[1:]),
            pltpu.SemaphoreType.DMA((len(small),)),
            pltpu.SemaphoreType.DMA((2, count)),
        ],

    )
    packs = [own, *partner_exchange(to_a, to_b)]

    fold = 2 if 2 * depth_local <= tile else 1
    more = -(-block // (16 * fold)) * 16
    early = max(1, count - 1)
    prepared = call(
        functools.partial(prepare_kernel, count, rows, momenta[0]), [coded] * (count + early), [near_estimate, near_previous]
    )
    currents = call(
        functools.partial(fill_kernel, count, rows, frames),
        [shape((rows * depth_local + 16 + more, tile), jnp.int16)] * count,
        [*packs, *prepared[:count]],
        scratch=[pltpu.VMEM((fold * more, tile), f32)],
    )
    (table,) = call(
        table_kernel,
        [shape(foot_table.shape, foot_table.dtype)],
        [foot_table],
        anchors=currents[:1],
    )
    currents = depth_exchange(currents)
    lanes = np.arange(prints * block)
    spread = jnp.asarray(lanes[None] % block == np.arange(block)[:, None], bf16)
    number = jnp.asarray(np.broadcast_to(lanes // block, (8, prints * block)), f32)
    sizes = (rows, block, frames, prints)
    acc = pltpu.VMEM((rows * block, tile), f32)
    part, double = shape((rows, frames, tile), f32), shape((2 * rows, frames, tile), f32)
    work = 2 * prints * block * width * (depth + tile)
    *parts, choose, ids = call(
        functools.partial(project_kernel, count, *sizes, depth_local),
        [double, double, part, part, shape((prints * block, depth), bf16), shape((block, depth), f32)],
        [*currents, table],
        scratch=[acc],
        flops=work,
    )
    (choose_t,) = call(
        functools.partial(choose_t_kernel, block, prints),
        [shape((depth, prints * block), bf16)],
        [spread, number, ids],
    )

    def exchange_parts(parts):
        return [*partner_exchange(*parts[:2]), *past_exchange(*parts[2:])]

    def step_sums(parts, received, hidden, late):
        to_a, part_b = parts[0], parts[3]
        gradient, sums = call(
            functools.partial(back_kernel, len(hidden), *sizes),
            [shape((depth, width), f32), shape((count * lat_count, tile), f32)],
            [
                *packs,
                to_a,
                part_b,
                *received,
                choose_t,
                table,
            ],
            scratch=[
                pltpu.VMEM((rows * block, tile), f32),
                pltpu.VMEM((prints * block, width), bf16),
                pltpu.VMEM((prints * block, width), bf16),
            ],
            flops=2 * work,
            anchors=hidden,
        )
        if late:
            (sums,) = call(pass_kernel, [shape(sums.shape, f32)], [sums], anchors=late)
        return gradient, lax.all_to_all(sums, ("lat", "dep"), split_axis=0, concat_axis=0, tiled=True)

    received = exchange_parts(parts)
    later = call(
        functools.partial(estimate_kernel, early, count, rows),
        [coded] * (count - early),
        [near_estimate],
        anchors=[received[0]],
    )
    states = depth_exchange([*prepared[count:], *later])
    gradient, sums = step_sums(parts, received, list(states[1:early]), states[early:])
    done = call(
        functools.partial(first_kernel, count, *sizes, depth_local, scale, momenta[1]),
        [double, double, part, part] + [shape((depth, width), f32)] * 2,
        [*currents, *states, sums, gradient, had, limits, choose, table],
        scratch=[acc],
        flops=work,
    )
    parts, current = done[:4], done[4]
    states = depth_exchange(
        call(functools.partial(state_kernel, rows, tile), [coded] * count, [done[5]])
    )
    gradient, sums = step_sums(parts, exchange_parts(parts), [], [])
    fresh = depth_exchange(
        call(
            functools.partial(last_kernel, count, rows, scale),
            [coded] * count,
            [sums, current, gradient, had, limits],
        )
    )
    return call(
        functools.partial(finish_kernel, count, rows, momenta[2]),
        [shape(estimate.shape, f32)] * 2,
        [*states, *fresh],
        far_outs=True,
        scratch=[
            pltpu.VMEM((count, *volume), f32),
            pltpu.VMEM((count, *volume), f32),
            pltpu.SemaphoreType.DMA((2, count)),
        ],
    )


def solution(mesh):
    in_specs = (
        P(None, "dep", "lat"),
        P(None, "dep", "lat"),
        P("dep", None, "lat"),
        P(),
        P("lat", None, "dep", None),
        P("lat", None, "dep"),
        P("lat", None, "dep"),
        P(),
        P(None, "lat"),
        P(),
    )
    out_specs = (P(None, "dep", "lat"), P(None, "dep", "lat"))
    return jax.shard_map(local, mesh=mesh, in_specs=in_specs, out_specs=out_specs, check_vma=False)
```
